256 devices in a mesh: dp: 16 (over z, core), expert: 16 (over x, y).
Axes of the slice: x: 4, y: 4, z: 8, core: 2. Of those that a mesh axis runs over, the one named last changes fastest.
Arguments:
- tokens: bfloat16 [32768, 2048], P(('dp', 'expert')), may hold values from -6 to 6
- expert_ids: int32 [32768, 2], P(('dp', 'expert')), may hold values from 0 to 15, as said below
- gate_weights: float32 [32768, 2], P(('dp', 'expert')), may hold values from 0.1 to 1
- w_gate: bfloat16 [16, 2048, 768], P('expert'), may hold values from -0.125 to 0.125
- w_up: bfloat16 [16, 2048, 768], P('expert'), may hold values from -0.125 to 0.125
- w_down: bfloat16 [16, 768, 2048], P('expert'), may hold values from -0.21875 to 0.21875
Outputs:
- mixed: bfloat16 [32768, 2048], P(('dp', 'expert'))
- aux_loss: float32 [], replicated
The draws below stay inside these ranges and needn't reach their ends.
Inputs may be any that keep to these rules, and one draw needn't show every extreme that they name: `expert_ids`: each token names 2 different experts. Two experts, the same two on every device, are each named exactly 48 times by the rows of every device; among the rows of one device every other expert is named at most 12 times, possibly not at all, and some other expert exactly 12 times.
All inputs are finite; a program needn't handle non-finite values.
Results may differ from the reference program's by a relative error of at most 0.0025.
The reference program's roundings to bfloat16 on the way count: a program that leaves them out, or rounds other values in their place, can miss the bound.
Values may be sent and summed in bfloat16 or wider, within the bound.
No kernel may reach another device: no remote copies, remote signals or barrier semaphores. Data moves between devices by JAX's collectives and lax.ppermute only.
A program may use at most 128 MiB of HBM per device.

```python
import jax
import jax.numpy as jnp
from jax import lax

D = 2048
FF = 768
EXP_DEV = 1
TOP = 2
TOK_DEV = 128
EXPERTS = 16
TOKENS = 32768
CAP = 48
CAP_COLD = 12
N_DP = 16
N_EXPERT = 16


def draw_expert_ids(key, part):
    key = jax.random.fold_in(key, 11)
    hot_key, rest_key = jax.random.split(key)
    order = jax.random.permutation(hot_key, EXPERTS).astype(jnp.int32)
    blocks = TOKENS // TOK_DEV
    picks = TOK_DEV * TOP
    cold = EXPERTS - 2
    remain = picks - 2 * CAP

    def one_block(block_key):
        count_key, token_key = jax.random.split(block_key)
        cold_rank = jax.random.permutation(count_key, cold).astype(jnp.int32)
        cold_counts = jnp.clip(remain - cold_rank * CAP_COLD, 0, CAP_COLD).astype(jnp.int32)
        counts = jnp.concatenate([jnp.full((2,), CAP, jnp.int32), cold_counts])
        bounds = jnp.cumsum(counts).astype(jnp.int32)
        position = jnp.arange(picks, dtype=jnp.int32)
        which = jnp.sum((position[:, None] >= bounds[None, :]).astype(jnp.int32), 1)
        sequence = order[which]
        pairs = sequence.reshape(TOP, TOK_DEV).T
        shuffle = jax.random.permutation(token_key, TOK_DEV)
        return pairs[shuffle]
    keys = jax.random.split(rest_key, blocks)
    return jax.vmap(one_block)(keys).reshape(TOKENS, TOP).astype(jnp.int32)


def draw_gate_weights(key, part):
    key = jax.random.fold_in(key, 23)
    group = EXPERTS // EXP_DEV
    blocks = TOKENS // TOK_DEV
    rows_dp = blocks // group
    block = jnp.arange(blocks, dtype=jnp.int32)
    dp_frac = (block // group).astype(jnp.float32) / float(max(rows_dp - 1, 1))
    ex_frac = (block % group).astype(jnp.float32) / float(max(group - 1, 1))
    base_level, rise_dp, rise_ex, low_end, high_end = (0.2, 2.5, 1.8, 0.6, 1.2)
    level = base_level * jnp.power(jnp.float32(rise_dp), dp_frac) * jnp.power(jnp.float32(rise_ex), ex_frac)
    noise = jax.random.uniform(key, (blocks, TOK_DEV, TOP), jnp.float32, low_end, high_end)
    gates = jnp.clip(level[:, None, None] * noise, 0.1, 1.0)
    return gates.reshape(TOKENS, TOP).astype(jnp.float32)


def level_of(key, dims, shards, smallest, high):
    factor_of = 1.0
    for dim, parts in shards:
        steps = jax.random.uniform(jax.random.fold_in(jax.random.fold_in(key, 6), dim), (parts,), jnp.float32, smallest / len(shards), high / len(shards))
        factor_of = factor_of * jnp.repeat(jnp.exp(steps), dims[dim] // parts).reshape((-1,) + (1,) * (len(dims) - 1 - dim))
    return factor_of


def scatter_about(stream_key, shape, scale, reach, shards=(), kind=jnp.bfloat16):
    factor_of = level_of(stream_key, shape, shards, -0.22, 0.18) if shards else 1.0
    array = jax.random.normal(stream_key, shape, jnp.float32) * scale * factor_of
    return jnp.minimum(jnp.maximum(array, -reach), reach).astype(kind)


def setup_inputs(seed: int = 0) -> dict:
    key_of = jax.random.split(jax.random.key(seed), 7)
    return {
        "tokens": scatter_about(key_of[0], (TOKENS, D), 1.0, 6.0, ((0, 256),)),
        "expert_ids": draw_expert_ids(jax.random.fold_in(key_of[6], 71), 0),
        "gate_weights": draw_gate_weights(jax.random.fold_in(key_of[6], 71), 0),
        "w_gate": scatter_about(key_of[3], (EXPERTS, D, FF), D ** -0.5, 0.125, ((0, 16),)),
        "w_up": scatter_about(key_of[4], (EXPERTS, D, FF), D ** -0.5, 0.125, ((0, 16),)),
        "w_down": scatter_about(key_of[5], (EXPERTS, FF, D), FF ** -0.5, 0.21875, ((0, 16),)),
    }


def run_expert(rows, gate_matrix, up_matrix, down_matrix):
    gate_part = jnp.dot(rows, gate_matrix, preferred_element_type=jnp.float32)
    up_part = jnp.dot(rows, up_matrix, preferred_element_type=jnp.float32)
    hidden = (jax.nn.silu(gate_part) * up_part).astype(jnp.bfloat16)
    return jnp.dot(hidden, down_matrix, preferred_element_type=jnp.float32).astype(jnp.bfloat16)


def reference(tokens, expert_ids, gate_weights, w_gate, w_up, w_down):
    flat_ids = expert_ids.reshape(-1).astype(jnp.int32)
    flat_gates = gate_weights.reshape(-1)
    row_count = flat_ids.shape[0]
    labels = jnp.arange(EXPERTS, dtype=jnp.int32)
    onehot = (flat_ids[:, None] == labels[None, :])
    load_all = jnp.sum(onehot.astype(jnp.float32), 0)
    mass_all = jnp.sum(jnp.where(onehot, flat_gates[:, None], jnp.float32(0.0)), 0)
    aux_loss = EXPERTS * jnp.sum(load_all / (TOKENS * TOP) * (mass_all / TOKENS))
    load_int = jnp.sum(onehot.astype(jnp.int32), 0)
    starts = (jnp.cumsum(load_int) - load_int).astype(jnp.int32)
    sorted_rows = jnp.argsort(flat_ids, stable=True).astype(jnp.int32)
    span_rows = min(TOKENS, N_DP * N_EXPERT * CAP)
    padded_token = jnp.concatenate([sorted_rows // TOP, jnp.zeros((span_rows,), jnp.int32)])
    padded_target = jnp.concatenate([sorted_rows, jnp.full((span_rows,), row_count, jnp.int32)])

    def one_expert(index, slot_out):
        token_index = lax.dynamic_slice_in_dim(padded_token, starts[index], span_rows)
        target_index = lax.dynamic_slice_in_dim(padded_target, starts[index], span_rows)
        is_valid = jnp.arange(span_rows, dtype=jnp.int32) < load_int[index]
        target_index = jnp.where(is_valid, target_index, row_count).astype(jnp.int32)
        result = run_expert(tokens[token_index], w_gate[index], w_up[index], w_down[index])
        return slot_out.at[target_index].set(result, mode="drop")

    slot_out = jnp.zeros((row_count + 1, D), jnp.bfloat16)
    slot_out = lax.fori_loop(0, EXPERTS, one_expert, slot_out)[:row_count]
    weighted = flat_gates[:, None] * slot_out.astype(jnp.float32)
    mixed = jnp.sum(weighted.reshape(TOKENS, TOP, D), 1).astype(jnp.bfloat16)
    return mixed, aux_loss
```

```python
import functools

import jax
import jax.numpy as jnp
from jax import lax
from jax.experimental import pallas as pl
from jax.experimental.pallas import tpu as pltpu
from jax.sharding import PartitionSpec as P

F32 = jnp.float32
BF16 = jnp.bfloat16
PARTS = 4


def pack_kernel(cap, ids_ref, gates_ref, tok_ref, out_ref, meta_ref, stats_ref, dest_ref):
    experts = stats_ref.shape[0]
    rows, toks = out_ref.shape[0], tok_ref.shape[0]
    step = pl.program_id(0)

    @pl.when(step == 0)
    def _():
        ids = ids_ref[...]
        gates = gates_ref[...]
        labels = lax.broadcasted_iota(jnp.int32, (experts, toks), 0)
        first = (labels == ids[0:1, :]).astype(F32)
        second = (labels == ids[1:2, :]).astype(F32)
        before = lax.broadcasted_iota(jnp.int32, (toks, toks), 0)
        after = lax.broadcasted_iota(jnp.int32, (toks, toks), 1)
        earlier = (before < after).astype(F32).astype(BF16)
        first_rank = jnp.dot(first.astype(BF16), earlier, preferred_element_type=F32)
        second_rank = jnp.dot(second.astype(BF16), earlier, preferred_element_type=F32)
        first_count = jnp.sum(first, 1, keepdims=True)
        count = first_count + jnp.sum(second, 1, keepdims=True)
        mass = jnp.sum(first * gates[0:1, :] + second * gates[1:2, :], 1, keepdims=True)
        base = ids.astype(F32) * cap
        first_dest = base[0:1, :] + jnp.sum(first * first_rank, 0, keepdims=True)
        second_dest = base[1:2, :] + jnp.sum(second * (second_rank + first_count), 0, keepdims=True)
        lanes = lax.broadcasted_iota(jnp.int32, stats_ref.shape, 1)
        stats_ref[...] = jnp.where(lanes == 0, count, jnp.where(lanes == 1, mass, 0.0))
        sub = lax.broadcasted_iota(jnp.int32, (toks, toks), 0)
        rows_up = jnp.where(sub == 0, first_dest, jnp.where(sub == 1, second_dest, 0.0))
        rows_up = jnp.where(sub == 2, gates[0:1, :], jnp.where(sub == 3, gates[1:2, :], rows_up))
        meta_ref[...] = rows_up.T
        dest_ref[0:1, :] = first_dest.astype(jnp.int32)
        dest_ref[1:2, :] = second_dest.astype(jnp.int32)

    slots = lax.broadcasted_iota(jnp.int32, (rows, toks), 0) + step * rows
    dest = dest_ref[...]
    pick = (slots == dest[0:1, :]) | (slots == dest[1:2, :])
    pick = pick.astype(F32).astype(BF16)
    out_ref[...] = jnp.dot(pick, tok_ref[...], preferred_element_type=F32).astype(BF16)


def pack(ids, gates, tokens, experts, cap):
    toks, width = tokens.shape
    slots = experts * cap
    rows = slots // PARTS
    whole = lambda shape: pl.BlockSpec(shape, lambda i: (0, 0))
    return pl.pallas_call(
        functools.partial(pack_kernel, cap),
        grid=(PARTS,),
        in_specs=[whole(ids.shape), whole(gates.shape), whole(tokens.shape)],
        out_specs=[
            pl.BlockSpec((rows, width), lambda i: (i, 0)),
            whole((toks, toks)),
            whole((experts, 128)),
        ],
        out_shape=[
            jax.ShapeDtypeStruct((slots, width), BF16),
            jax.ShapeDtypeStruct((toks, toks), F32),
            jax.ShapeDtypeStruct((experts, 128), F32),
        ],
        scratch_shapes=[pltpu.VMEM((8, toks), jnp.int32)],
        compiler_params=pltpu.CompilerParams(vmem_limit_bytes=16 * 2**20),
        cost_estimate=pl.CostEstimate(
            flops=2 * slots * toks * width, bytes_accessed=4 * slots * width, transcendentals=0
        ),
        name="pack",
    )(ids, gates, tokens)


def hidden_kernel(x_ref, gate_ref, up_ref, out_ref):
    x = x_ref[...]
    gate = jnp.dot(x, gate_ref[0], preferred_element_type=F32)
    up = jnp.dot(x, up_ref[0], preferred_element_type=F32)
    out_ref[...] = (gate / (1.0 + jnp.exp(-gate)) * up).astype(BF16)


def down_kernel(x_ref, down_ref, out_ref):
    out_ref[...] = jnp.dot(x_ref[...], down_ref[0], preferred_element_type=F32).astype(BF16)


def rows_kernel(body, x, weights, out_width, block, name):
    rows, width = x.shape
    once = pl.Buffered(1)
    return pl.pallas_call(
        body,
        grid=(rows // block,),
        in_specs=[pl.BlockSpec((block, width), lambda i: (i, 0))]
        + [pl.BlockSpec(w.shape, lambda i: (0, 0, 0), pipeline_mode=once) for w in weights],
        out_specs=pl.BlockSpec((block, out_width), lambda i: (i, 0)),
        out_shape=jax.ShapeDtypeStruct((rows, out_width), BF16),
        compiler_params=pltpu.CompilerParams(vmem_limit_bytes=24 * 2**20),
        cost_estimate=pl.CostEstimate(
            flops=2 * rows * width * out_width * len(weights),
            bytes_accessed=2 * (rows * (width + out_width) + len(weights) * width * out_width),
            transcendentals=0,
        ),
        name=name,
    )(x, *weights)


def combine_kernel(meta_ref, rows_ref, out_ref, pick_ref):
    toks = out_ref.shape[0]
    slots = rows_ref.shape[0]

    @pl.when(pl.program_id(0) == 0)
    def _():
        dest = meta_ref[:, 0:2].astype(jnp.int32)
        lane = lax.broadcasted_iota(jnp.int32, (toks, slots), 1)
        pick_ref[:toks, :] = (lane == dest[:, 0:1]).astype(F32).astype(BF16)
        pick_ref[toks:, :] = (lane == dest[:, 1:2]).astype(F32).astype(BF16)

    both = jnp.dot(pick_ref[...], rows_ref[...], preferred_element_type=F32)
    weights = meta_ref[:, 2:4]
    out_ref[...] = (weights[:, 0:1] * both[:toks] + weights[:, 1:2] * both[toks:]).astype(BF16)


def combine(meta, rows):
    toks = meta.shape[0]
    slots, width = rows.shape
    block = width // PARTS
    return pl.pallas_call(
        combine_kernel,
        grid=(PARTS,),
        in_specs=[
            pl.BlockSpec(meta.shape, lambda i: (0, 0)),
            pl.BlockSpec((slots, block), lambda i: (0, i)),
        ],
        out_specs=pl.BlockSpec((toks, block), lambda i: (0, i)),
        out_shape=jax.ShapeDtypeStruct((toks, width), BF16),
        scratch_shapes=[pltpu.VMEM((2 * toks, slots), BF16)],
        compiler_params=pltpu.CompilerParams(vmem_limit_bytes=16 * 2**20),
        cost_estimate=pl.CostEstimate(
            flops=4 * toks * slots * width, bytes_accessed=2 * slots * width, transcendentals=0
        ),
        name="combine",
    )(meta, rows)


def radix_sum(value, axis, size, stride):
    total = value
    for turn in range(1, 4):
        pairs = []
        for i in range(size):
            digit = (i // stride) % 4
            pairs.append((i, i + ((digit + turn) % 4 - digit) * stride))
        total = total + lax.ppermute(value, axis, pairs)
    return total


def on_device(tokens, expert_ids, gate_weights, w_gate, w_up, w_down):
    toks, width = tokens.shape
    picks = expert_ids.shape[1]
    group = lax.axis_size("expert")
    copies = lax.axis_size("dp")
    experts = w_gate.shape[0] * group
    cap = min(toks * picks // 4, 3 * toks * picks // experts)
    all_tokens = toks * group * copies

    outgoing, meta, stats = pack(expert_ids.T, gate_weights.T, tokens, experts, cap)
    stats = radix_sum(stats, "expert", group, 1)
    received = lax.all_to_all(outgoing, "expert", split_axis=0, concat_axis=0, tiled=True)
    stats, received = lax.optimization_barrier((stats, received))
    stats = radix_sum(stats, "expert", group, 4)
    hidden = rows_kernel(hidden_kernel, received, (w_gate, w_up), w_gate.shape[2], 256, "hidden")
    stats, hidden = lax.optimization_barrier((stats, hidden))
    stats = radix_sum(stats, "dp", copies, 1)
    result = rows_kernel(down_kernel, hidden, (w_down,), width, 256, "down")
    stats, result = lax.optimization_barrier((stats, result))
    stats = radix_sum(stats, "dp", copies, 4)
    returned = lax.all_to_all(result, "expert", split_axis=0, concat_axis=0, tiled=True)
    stats, returned = lax.optimization_barrier((stats, returned))
    mixed = combine(meta, returned)
    load, mass = stats[:, 0], stats[:, 1]
    aux_loss = experts * jnp.sum(load / (all_tokens * picks) * (mass / all_tokens))
    return mixed, aux_loss


def solution(mesh):
    rows = P(("dp", "expert"), None)
    held = P("expert", None, None)
    return jax.shard_map(
        on_device,
        mesh=mesh,
        in_specs=(rows, rows, rows, held, held, held),
        out_specs=(rows, P()),
        check_vma=False,
    )
```

```python
import functools

import jax
import jax.numpy as jnp
from jax import lax
from jax.experimental import pallas as pl
from jax.experimental.pallas import tpu as pltpu
from jax.sharding import PartitionSpec as P

F32 = jnp.float32
BF16 = jnp.bfloat16
PARTS = 4
PACK_VMEM = 60 * 2**20


def pack_kernel(cap, ids_ref, gates_ref, tok_ref, out_ref, meta_ref, dest_ref, note_ref):
    rows, toks = out_ref.shape[0], tok_ref.shape[0]
    experts = rows * PARTS // cap
    step = pl.program_id(0)

    @pl.when(step == 0)
    def _():
        ids = ids_ref[...]
        gates = gates_ref[...]
        labels = lax.broadcasted_iota(jnp.int32, (toks, toks), 0)
        first = (labels == ids[0:1, :]).astype(F32)
        second = (labels == ids[1:2, :]).astype(F32)
        lanes = lax.broadcasted_iota(jnp.int32, (toks, toks), 1)
        earlier = (labels < lanes).astype(F32).astype(BF16)
        first_rank = jnp.dot(first.astype(BF16), earlier, preferred_element_type=F32)
        second_rank = jnp.dot(second.astype(BF16), earlier, preferred_element_type=F32)
        first_count = jnp.sum(first, 1, keepdims=True)
        count = first_count + jnp.sum(second, 1, keepdims=True)
        mass = jnp.sum(first * gates[0:1, :] + second * gates[1:2, :], 1, keepdims=True)
        base = ids.astype(F32) * cap
        first_dest = base[0:1, :] + jnp.sum(first * first_rank, 0, keepdims=True)
        second_dest = base[1:2, :] + jnp.sum(second * (second_rank + first_count), 0, keepdims=True)
        dest_ref[0:1, :] = first_dest.astype(jnp.int32)
        dest_ref[1:2, :] = second_dest.astype(jnp.int32)
        high = mass.astype(BF16).astype(F32)
        middle = (mass - high).astype(BF16).astype(F32)
        low = mass - high - middle
        columns = jnp.where(lanes == 0, count, jnp.where(lanes == 1, high, 0.0))
        columns = jnp.where(lanes == 2, middle, jnp.where(lanes == 3, low, columns))
        lines = columns.T
        free = (count < cap) & (labels < experts)
        for i in range(4):
            line = jnp.where(free, lines[i : i + 1, :], 0.0)
            note_ref[:, i * toks : (i + 1) * toks] = line.astype(BF16)
        expert = lax.broadcasted_iota(jnp.int32, (toks, 1), 0).astype(F32)
        slot = jnp.where((count < cap) & (expert < experts), expert * cap + (cap - 1), 1e6)
        slot = jnp.min(slot, 0, keepdims=True)
        lines = jnp.where(labels == 0, first_dest, jnp.where(labels == 1, second_dest, 0.0))
        lines = jnp.where(labels == 2, gates[0:1, :], jnp.where(labels == 3, gates[1:2, :], lines))
        lines = jnp.where(labels == 4, slot, lines)
        meta_ref[...] = jnp.where(lanes == 5, free.astype(F32), lines.T)

    slots = lax.broadcasted_iota(jnp.int32, (rows, toks), 0) + step * rows
    lanes = lax.broadcasted_iota(jnp.int32, (rows, toks), 1)
    dest = dest_ref[...]
    pick = (slots == dest[0:1, :]) | (slots == dest[1:2, :])
    pick = pick.astype(F32).astype(BF16)
    last = (slots == lanes * cap + (cap - 1)).astype(F32).astype(BF16)
    edge = note_ref.shape[1]
    head = jnp.dot(pick, tok_ref[:, :edge], preferred_element_type=F32)
    head = head + jnp.dot(last, note_ref[...], preferred_element_type=F32)
    out_ref[:, :edge] = head.astype(BF16)
    out_ref[:, edge:] = jnp.dot(pick, tok_ref[:, edge:], preferred_element_type=F32).astype(BF16)


def pack(ids, gates, tokens, experts, cap):
    toks, width = tokens.shape
    slots = experts * cap
    rows = slots // PARTS
    whole = lambda shape: pl.BlockSpec(shape, lambda i: (0, 0))
    return pl.pallas_call(
        functools.partial(pack_kernel, cap),
        grid=(PARTS,),
        in_specs=[whole(ids.shape), whole(gates.shape), whole(tokens.shape)],
        out_specs=[
            pl.BlockSpec((rows, width), lambda i: (i, 0)),
            whole((toks, toks)),
        ],
        out_shape=[
            jax.ShapeDtypeStruct((slots, width), BF16),
            jax.ShapeDtypeStruct((toks, toks), F32),
        ],
        scratch_shapes=[pltpu.VMEM((8, toks), jnp.int32), pltpu.VMEM((toks, 4 * toks), BF16)],
        compiler_params=pltpu.CompilerParams(vmem_limit_bytes=PACK_VMEM),
        cost_estimate=pl.CostEstimate(
            flops=2 * slots * toks * width, bytes_accessed=4 * slots * width, transcendentals=0
        ),
        name="pack",
    )(ids, gates, tokens)


def hidden_kernel(x_ref, gate_ref, up_ref, out_ref):
    x = x_ref[...]
    gate = jnp.dot(x, gate_ref[0], preferred_element_type=F32)
    up = jnp.dot(x, up_ref[0], preferred_element_type=F32)
    out_ref[...] = (gate / (1.0 + jnp.exp(-gate)) * up).astype(BF16)


def down_kernel(x_ref, down_ref, out_ref):
    out_ref[...] = jnp.dot(x_ref[...], down_ref[0], preferred_element_type=F32).astype(BF16)


def rows_kernel(body, x, weights, out_width, block, name):
    rows, width = x.shape
    once = pl.Buffered(1)
    return pl.pallas_call(
        body,
        grid=(rows // block,),
        in_specs=[pl.BlockSpec((block, width), lambda i: (i, 0))]
        + [pl.BlockSpec(w.shape, lambda i: (0, 0, 0), pipeline_mode=once) for w in weights],
        out_specs=pl.BlockSpec((block, out_width), lambda i: (i, 0)),
        out_shape=jax.ShapeDtypeStruct((rows, out_width), BF16),
        compiler_params=pltpu.CompilerParams(vmem_limit_bytes=24 * 2**20),
        cost_estimate=pl.CostEstimate(
            flops=2 * rows * width * out_width * len(weights),
            bytes_accessed=2 * (rows * (width + out_width) + len(weights) * width * out_width),
            transcendentals=0,
        ),
        name=name,
    )(x, *weights)


def combine_kernel(meta_ref, rows_ref, out_ref, note_ref, pick_ref):
    toks = out_ref.shape[0]
    slots = rows_ref.shape[0]

    @pl.when(pl.program_id(0) == 0)
    def _():
        dest = meta_ref[:, 0:5].astype(jnp.int32)
        lane = lax.broadcasted_iota(jnp.int32, (toks, slots), 1)
        pick_ref[:toks, :] = (lane == dest[:, 0:1]).astype(F32).astype(BF16)
        pick_ref[toks:, :] = (lane == dest[:, 1:2]).astype(F32).astype(BF16)
        slot = (lane[:16, :] == dest[:16, 4:5]).astype(F32).astype(BF16)
        note = jnp.dot(slot, rows_ref[:, :128], preferred_element_type=F32)
        note_ref[...] = note[:8, :]

    both = jnp.dot(pick_ref[...], rows_ref[...], preferred_element_type=F32)
    weights = meta_ref[:, 2:4]
    out_ref[...] = (weights[:, 0:1] * both[:toks] + weights[:, 1:2] * both[toks:]).astype(BF16)


def combine(meta, rows):
    toks = meta.shape[0]
    slots, width = rows.shape
    block = width // PARTS
    return pl.pallas_call(
        combine_kernel,
        grid=(PARTS,),
        in_specs=[
            pl.BlockSpec(meta.shape, lambda i: (0, 0)),
            pl.BlockSpec((slots, block), lambda i: (0, i)),
        ],
        out_specs=[
            pl.BlockSpec((toks, block), lambda i: (0, i)),
            pl.BlockSpec((8, 128), lambda i: (0, 0)),
        ],
        out_shape=[
            jax.ShapeDtypeStruct((toks, width), BF16),
            jax.ShapeDtypeStruct((8, 128), F32),
        ],
        scratch_shapes=[pltpu.VMEM((2 * toks, slots), BF16)],
        compiler_params=pltpu.CompilerParams(vmem_limit_bytes=16 * 2**20),
        cost_estimate=pl.CostEstimate(
            flops=4 * toks * slots * width, bytes_accessed=2 * slots * width, transcendentals=0
        ),
        name="combine",
    )(meta, rows)


def radix_sum(value, axis, size, stride):
    total = value
    for turn in range(1, 4):
        pairs = []
        for i in range(size):
            digit = (i // stride) % 4
            pairs.append((i, i + ((digit + turn) % 4 - digit) * stride))
        total = total + lax.ppermute(value, axis, pairs)
    return total


def on_device(tokens, expert_ids, gate_weights, w_gate, w_up, w_down):
    toks, width = tokens.shape
    picks = expert_ids.shape[1]
    group = lax.axis_size("expert")
    copies = lax.axis_size("dp")
    experts = w_gate.shape[0] * group
    cap = min(toks * picks // 4, 3 * toks * picks // experts)
    all_tokens = toks * group * copies

    outgoing, meta = pack(expert_ids.T, gate_weights.T, tokens, experts, cap)
    received = lax.all_to_all(outgoing, "expert", split_axis=0, concat_axis=0, tiled=True)

    notes = received.reshape(group, cap, width)[:, cap - 1, : 4 * toks].astype(F32)
    notes = jnp.sum(notes, 0).reshape(4, toks)
    stats = jnp.concatenate([notes[0:1], notes[1:2] + notes[2:3] + notes[3:4]])
    stats, received = lax.optimization_barrier((stats, received))
    stats = radix_sum(stats, "dp", copies, 1)
    hidden = rows_kernel(hidden_kernel, received, (w_gate, w_up), w_gate.shape[2], 256, "hidden")
    stats, hidden = lax.optimization_barrier((stats, hidden))
    stats = radix_sum(stats, "dp", copies, 4)
    result = rows_kernel(down_kernel, hidden, (w_down,), width, 256, "down")
    stats, result = lax.optimization_barrier((stats, result))

    load, mass = stats[0, :experts], stats[1, :experts]
    mine = lax.axis_index("expert")
    aux_loss = experts * jnp.sum(load / (all_tokens * picks) * (mass / all_tokens))
    high = aux_loss.astype(BF16)
    middle = (aux_loss - high.astype(F32)).astype(BF16)
    low = (aux_loss - high.astype(F32) - middle.astype(F32)).astype(BF16)
    lanes = lax.broadcasted_iota(jnp.int32, (1, 1, toks), 2)
    line = jnp.where(lanes == 0, high, jnp.where(lanes == 1, middle, jnp.where(lanes == 2, low, BF16(0))))
    result = result.reshape(group, cap, width)
    last = result[:, cap - 1 :, :toks]
    is_free = meta[mine, 5] > 0
    line = jnp.where(is_free, line, last)
    result = lax.dynamic_update_slice(result, line, (0, cap - 1, 0)).reshape(experts * cap, width)

    returned = lax.all_to_all(result, "expert", split_axis=0, concat_axis=0, tiled=True)
    mixed, note = combine(meta, returned)
    return mixed, note[0, 0] + note[0, 1] + note[0, 2]


def solution(mesh):
    rows = P(("dp", "expert"), None)
    held = P("expert", None, None)
    return jax.shard_map(
        on_device,
        mesh=mesh,
        in_specs=(rows, rows, rows, held, held, held),
        out_specs=(rows, P()),
        check_vma=False,
    )
```

```python
import functools

import jax
import jax.numpy as jnp
from jax import lax
from jax.experimental import pallas as pl
from jax.experimental.pallas import tpu as pltpu
from jax.sharding import PartitionSpec as P

F32 = jnp.float32
BF16 = jnp.bfloat16
PARTS = 4
AXES = ("dp", "expert")


def pack_kernel(cap, ids_hbm, gates_hbm, tok_hbm, out_ref, meta_ref, stats_ref, ids_ref, gates_ref, tok_ref, sems):
    slots, toks = out_ref.shape[0], tok_ref.shape[0]
    rows = slots // PARTS
    ids_copy = pltpu.make_async_copy(ids_hbm, ids_ref, sems.at[0])
    gates_copy = pltpu.make_async_copy(gates_hbm, gates_ref, sems.at[1])
    tok_copy = pltpu.make_async_copy(tok_hbm, tok_ref, sems.at[2])
    ids_copy.start()
    gates_copy.start()
    tok_copy.start()
    ids_copy.wait()
    gates_copy.wait()

    ids = ids_ref[...]
    gates = gates_ref[...]
    labels = lax.broadcasted_iota(jnp.int32, (toks, toks), 0)
    lanes = lax.broadcasted_iota(jnp.int32, (toks, toks), 1)
    first = (labels == ids[0:1, :]).astype(F32)
    second = (labels == ids[1:2, :]).astype(F32)
    earlier = (labels < lanes).astype(F32).astype(BF16)
    first_rank = jnp.dot(first.astype(BF16), earlier, preferred_element_type=F32)
    second_rank = jnp.dot(second.astype(BF16), earlier, preferred_element_type=F32)
    first_count = jnp.sum(first, 1, keepdims=True)
    count = first_count + jnp.sum(second, 1, keepdims=True)
    mass = jnp.sum(first * gates[0:1, :] + second * gates[1:2, :], 1, keepdims=True)
    base = ids.astype(F32) * cap
    first_dest = base[0:1, :] + jnp.sum(first * first_rank, 0, keepdims=True)
    second_dest = base[1:2, :] + jnp.sum(second * (second_rank + first_count), 0, keepdims=True)
    stats_ref[...] = jnp.where(lanes == 0, count, jnp.where(lanes == 1, mass, 0.0)).T[:8, :]
    lines = jnp.where(labels == 0, first_dest, jnp.where(labels == 1, second_dest, 0.0))
    lines = jnp.where(labels == 2, gates[0:1, :], jnp.where(labels == 3, gates[1:2, :], lines))
    meta_ref[...] = lines.T

    tok_copy.wait()
    tokens = tok_ref[...]
    for part in range(PARTS):
        slot = lax.broadcasted_iota(jnp.int32, (rows, toks), 0) + part * rows
        pick = (slot == first_dest.astype(jnp.int32)) | (slot == second_dest.astype(jnp.int32))
        pick = pick.astype(F32).astype(BF16)
        out_ref[part * rows : (part + 1) * rows, :] = jnp.dot(
            pick, tokens, preferred_element_type=F32
        ).astype(BF16)


def pack(ids, gates, tokens, experts, cap):
    toks, width = tokens.shape
    slots = experts * cap
    return pl.pallas_call(
        functools.partial(pack_kernel, cap),
        in_specs=[pl.BlockSpec(memory_space=pltpu.HBM)] * 3,
        out_specs=[pl.BlockSpec(memory_space=pltpu.VMEM)] * 3,
        out_shape=[
            jax.ShapeDtypeStruct((slots, width), BF16),
            jax.ShapeDtypeStruct((toks, toks), F32),
            jax.ShapeDtypeStruct((8, toks), F32),
        ],
        scratch_shapes=[
            pltpu.VMEM(ids.shape, ids.dtype),
            pltpu.VMEM(gates.shape, gates.dtype),
            pltpu.VMEM(tokens.shape, tokens.dtype),
            pltpu.SemaphoreType.DMA((3,)),
        ],
        compiler_params=pltpu.CompilerParams(vmem_limit_bytes=16 * 2**20),
        cost_estimate=pl.CostEstimate(
            flops=2 * slots * toks * width, bytes_accessed=4 * slots * width, transcendentals=0
        ),
        name="pack",
    )(*(pltpu.with_memory_space_constraint(a, pltpu.HBM) for a in (ids, gates, tokens)))


def ffn_kernel(x_ref, gate_ref, up_ref, down_ref, out_ref):
    x = x_ref[...]
    gate = jnp.dot(x, gate_ref[0], preferred_element_type=F32)
    up = jnp.dot(x, up_ref[0], preferred_element_type=F32)
    hidden = (gate / (1.0 + jnp.exp(-gate)) * up).astype(BF16)
    out_ref[...] = jnp.dot(hidden, down_ref[0], preferred_element_type=F32).astype(BF16)


def ffn(x, w_gate, w_up, w_down):
    rows, width = x.shape
    middle = w_gate.shape[2]
    block = rows // 3
    held = pl.BlockSpec(memory_space=pltpu.VMEM)
    return pl.pallas_call(
        ffn_kernel,
        grid=(3,),
        in_specs=[pl.BlockSpec((block, width), lambda i: (i, 0)), held, held, held],
        out_specs=pl.BlockSpec((block, width), lambda i: (i, 0)),
        out_shape=pltpu.HBM((rows, width), BF16),
        compiler_params=pltpu.CompilerParams(vmem_limit_bytes=32 * 2**20),
        cost_estimate=pl.CostEstimate(
            flops=6 * rows * width * middle,
            bytes_accessed=4 * rows * width + 6 * width * middle,
            transcendentals=rows * middle,
        ),
        name="ffn",
    )(x, w_gate, w_up, w_down)


def combine_kernel(meta_ref, rows_ref, out_ref, pick_ref):
    toks = out_ref.shape[0]
    slots = rows_ref.shape[0]

    @pl.when(pl.program_id(0) == 0)
    def _():
        dest = meta_ref[:, 0:2].astype(jnp.int32)
        lane = lax.broadcasted_iota(jnp.int32, (toks, slots), 1)
        pick_ref[:toks, :] = (lane == dest[:, 0:1]).astype(F32).astype(BF16)
        pick_ref[toks:, :] = (lane == dest[:, 1:2]).astype(F32).astype(BF16)

    both = jnp.dot(pick_ref[...], rows_ref[...], preferred_element_type=F32)
    weights = meta_ref[:, 2:4]
    out_ref[...] = (weights[:, 0:1] * both[:toks] + weights[:, 1:2] * both[toks:]).astype(BF16)


def combine(meta, rows):
    toks = meta.shape[0]
    slots, width = rows.shape
    block = width // PARTS
    return pl.pallas_call(
        combine_kernel,
        grid=(PARTS,),
        in_specs=[
            pl.BlockSpec(meta.shape, lambda i: (0, 0)),
            pl.BlockSpec((slots, block), lambda i: (0, i)),
        ],
        out_specs=pl.BlockSpec((toks, block), lambda i: (0, i)),
        out_shape=jax.ShapeDtypeStruct((toks, width), BF16),
        scratch_shapes=[pltpu.VMEM((2 * toks, slots), BF16)],
        compiler_params=pltpu.CompilerParams(vmem_limit_bytes=16 * 2**20),
        cost_estimate=pl.CostEstimate(
            flops=4 * toks * slots * width, bytes_accessed=2 * slots * width, transcendentals=0
        ),
        name="combine",
    )(meta, rows)


def add_round(value, size, stride, step):
    return value + lax.ppermute(value, AXES, [(i, i ^ stride) for i in range(size) if (i // step) % 2 == 1])


def hand_over(value, size, step, sender):
    turn = step if sender == 0 else -step
    return lax.ppermute(value, AXES, [(i, i + turn) for i in range(size) if (i // step) % 2 == sender])


def on_device(tokens, expert_ids, gate_weights, w_gate, w_up, w_down):
    toks, width = tokens.shape
    picks = expert_ids.shape[1]
    group = lax.axis_size("expert")
    copies = lax.axis_size("dp")
    experts = w_gate.shape[0] * group
    cap = min(toks * picks // 4, 3 * toks * picks // experts)
    all_tokens = toks * group * copies

    size = copies * group
    stride = 2 * group
    outgoing, meta, stats = pack(expert_ids.T, gate_weights.T, tokens, experts, cap)
    stats = stats + hand_over(stats, size, group, 0)
    for bit in (1, 2, 4, 8):
        stats = add_round(stats, size, bit, group)
    stats, outgoing = lax.optimization_barrier((stats, outgoing))
    received = lax.all_to_all(outgoing, "expert", split_axis=0, concat_axis=0, tiled=True)
    result = ffn(received, w_gate, w_up, w_down)
    stats, result = lax.optimization_barrier((stats, result))
    returned = lax.all_to_all(result, "expert", split_axis=0, concat_axis=0, tiled=True)
    for bit in (stride, 2 * stride, 4 * stride):
        stats = add_round(stats, size, bit, group)
    stats = jnp.where(lax.axis_index("dp") % 2 == 1, stats, hand_over(stats, size, group, 1))
    load, mass = stats[0, :experts], stats[1, :experts]
    aux_loss = experts * jnp.sum(load / (all_tokens * picks) * (mass / all_tokens))
    return combine(meta, returned), aux_loss


def solution(mesh):
    rows = P(("dp", "expert"), None)
    held = P("expert", None, None)
    return jax.shard_map(
        on_device,
        mesh=mesh,
        in_specs=(rows, rows, rows, held, held, held),
        out_specs=(rows, P()),
        check_vma=False,
    )
```

```python
import functools

import jax
import jax.numpy as jnp
from jax import lax
from jax.experimental import pallas as pl
from jax.experimental.pallas import tpu as pltpu
from jax.sharding import PartitionSpec as P

F32 = jnp.float32
BF16 = jnp.bfloat16
PARTS = 4
AXES = ("dp", "expert")


def slots_of(ids, cap):
    toks = ids.shape[1]
    labels = lax.broadcasted_iota(jnp.int32, (toks, toks), 0)
    lanes = lax.broadcasted_iota(jnp.int32, (toks, toks), 1)
    first = (labels == ids[0:1, :]).astype(F32)
    second = (labels == ids[1:2, :]).astype(F32)
    earlier = (labels < lanes).astype(F32).astype(BF16)
    first_rank = jnp.dot(first.astype(BF16), earlier, preferred_element_type=F32)
    second_rank = jnp.dot(second.astype(BF16), earlier, preferred_element_type=F32)
    first_count = jnp.sum(first, 1, keepdims=True)
    base = ids.astype(F32) * cap
    first_slot = base[0:1, :] + jnp.sum(first * first_rank, 0, keepdims=True)
    second_slot = base[1:2, :] + jnp.sum(second * (second_rank + first_count), 0, keepdims=True)
    return first_slot, second_slot, first, second


def pack_kernel(cap, ids_hbm, gates_hbm, tok_hbm, out_ref, stats_ref, ids_ref, gates_ref, tok_ref, sems):
    slots, toks = out_ref.shape[0], tok_ref.shape[0]
    rows = slots // PARTS
    ids_copy = pltpu.make_async_copy(ids_hbm, ids_ref, sems.at[0])
    gates_copy = pltpu.make_async_copy(gates_hbm, gates_ref, sems.at[1])
    tok_copy = pltpu.make_async_copy(tok_hbm, tok_ref, sems.at[2])
    ids_copy.start()
    gates_copy.start()
    tok_copy.start()
    ids_copy.wait()
    gates_copy.wait()

    gates = gates_ref[...]
    first_slot, second_slot, first, second = slots_of(ids_ref[...], cap)
    count = jnp.sum(first + second, 1, keepdims=True)
    mass = jnp.sum(first * gates[0:1, :] + second * gates[1:2, :], 1, keepdims=True)
    lanes = lax.broadcasted_iota(jnp.int32, (toks, toks), 1)
    stats_ref[...] = jnp.where(lanes == 0, count, jnp.where(lanes == 1, mass, 0.0)).T[:8, :]

    tok_copy.wait()
    tokens = tok_ref[...]
    first_slot, second_slot = first_slot.astype(jnp.int32), second_slot.astype(jnp.int32)
    for part in range(PARTS):
        slot = lax.broadcasted_iota(jnp.int32, (rows, toks), 0) + part * rows
        pick = ((slot == first_slot) | (slot == second_slot)).astype(F32).astype(BF16)
        out_ref[part * rows : (part + 1) * rows, :] = jnp.dot(
            pick, tokens, preferred_element_type=F32
        ).astype(BF16)


def pack(ids, gates, tokens, experts, cap):
    toks, width = tokens.shape
    slots = experts * cap
    return pl.pallas_call(
        functools.partial(pack_kernel, cap),
        in_specs=[pl.BlockSpec(memory_space=pltpu.HBM)] * 3,
        out_specs=[pl.BlockSpec(memory_space=pltpu.VMEM)] * 2,
        out_shape=[
            jax.ShapeDtypeStruct((slots, width), BF16),
            jax.ShapeDtypeStruct((8, toks), F32),
        ],
        scratch_shapes=[
            pltpu.VMEM(ids.shape, ids.dtype),
            pltpu.VMEM(gates.shape, gates.dtype),
            pltpu.VMEM(tokens.shape, tokens.dtype),
            pltpu.SemaphoreType.DMA((3,)),
        ],
        compiler_params=pltpu.CompilerParams(vmem_limit_bytes=16 * 2**20),
        cost_estimate=pl.CostEstimate(
            flops=2 * slots * toks * width, bytes_accessed=4 * slots * width, transcendentals=0
        ),
        name="pack",
    )(*(pltpu.with_memory_space_constraint(a, pltpu.HBM) for a in (ids, gates, tokens)))


def hidden_kernel(x_ref, gate_ref, up_ref, out_ref):
    x = x_ref[...]
    for start in range(0, out_ref.shape[1], 256):
        tile = slice(start, start + 256)
        gate = jnp.dot(x, gate_ref[0, :, tile], preferred_element_type=F32)
        up = jnp.dot(x, up_ref[0, :, tile], preferred_element_type=F32)
        out_ref[:, tile] = (gate / (1.0 + jnp.exp(-gate)) * up).astype(BF16)


def hidden_of(x, w_gate, w_up):
    rows, width = x.shape
    middle = w_gate.shape[2]
    held = pl.BlockSpec(memory_space=pltpu.VMEM)
    return pl.pallas_call(
        hidden_kernel,
        in_specs=[held] * 3,
        out_specs=held,
        out_shape=jax.ShapeDtypeStruct((rows, middle), BF16),
        compiler_params=pltpu.CompilerParams(vmem_limit_bytes=16 * 2**20),
        cost_estimate=pl.CostEstimate(
            flops=4 * rows * width * middle,
            bytes_accessed=2 * rows * width + 4 * width * middle,
            transcendentals=rows * middle,
        ),
        name="hidden",
    )(x, w_gate, w_up)


def down_kernel(x_ref, down_ref, out_hbm, out_ref, sems):
    copies = []
    for part in range(sems.shape[0]):
        tile = pl.ds(part * 256, 256)
        out_ref[tile, :] = jnp.dot(
            x_ref[tile, :], down_ref[0], preferred_element_type=F32
        ).astype(BF16)
        copies.append(pltpu.make_async_copy(out_ref.at[tile], out_hbm.at[tile], sems.at[part]))
        copies[-1].start()
    for copy in copies:
        copy.wait()


def down_of(x, w_down):
    rows, middle = x.shape
    width = w_down.shape[2]
    held = pl.BlockSpec(memory_space=pltpu.VMEM)
    return pl.pallas_call(
        down_kernel,
        in_specs=[held] * 2,
        out_specs=pl.BlockSpec(memory_space=pltpu.HBM),
        out_shape=pltpu.HBM((rows, width), BF16),
        scratch_shapes=[pltpu.VMEM((rows, width), BF16), pltpu.SemaphoreType.DMA((rows // 256,))],
        compiler_params=pltpu.CompilerParams(vmem_limit_bytes=16 * 2**20),
        cost_estimate=pl.CostEstimate(
            flops=2 * rows * width * middle,
            bytes_accessed=2 * rows * width + 2 * width * middle,
            transcendentals=0,
        ),
        name="down",
    )(x, w_down)


def select_kernel(cap, ids_ref, pick_ref):
    toks, slots = ids_ref.shape[1], pick_ref.shape[1]
    first_slot, second_slot, _, _ = slots_of(ids_ref[...], cap)
    labels = lax.broadcasted_iota(jnp.int32, (toks, toks), 0)
    lines = jnp.where(labels == 0, first_slot, jnp.where(labels == 1, second_slot, 0.0)).T
    dest = lines[:, 0:2].astype(jnp.int32)
    lane = lax.broadcasted_iota(jnp.int32, (toks, slots), 1)
    pick_ref[:toks, :] = (lane == dest[:, 0:1]).astype(F32).astype(BF16)
    pick_ref[toks:, :] = (lane == dest[:, 1:2]).astype(F32).astype(BF16)


def select(ids, slots, cap):
    toks = ids.shape[1]
    held = pl.BlockSpec(memory_space=pltpu.VMEM)
    return pl.pallas_call(
        functools.partial(select_kernel, cap),
        in_specs=[held],
        out_specs=held,
        out_shape=jax.ShapeDtypeStruct((2 * toks, slots), BF16),
        compiler_params=pltpu.CompilerParams(vmem_limit_bytes=4 * 2**20),
        cost_estimate=pl.CostEstimate(flops=0, bytes_accessed=4 * toks * slots, transcendentals=0),
        name="select",
    )(ids)


def combine_kernel(pick_ref, gates_ref, rows_ref, out_hbm, out_ref, sems):
    toks, width = out_ref.shape
    gates = gates_ref[...]
    labels = lax.broadcasted_iota(jnp.int32, (toks, toks), 0)
    lines = jnp.where(labels == 0, gates[0:1, :], jnp.where(labels == 1, gates[1:2, :], 0.0)).T
    first, second = lines[:, 0:1], lines[:, 1:2]
    block = width // PARTS
    copies = []
    for part in range(PARTS):
        tile = pl.ds(part * block, block)
        both = jnp.dot(pick_ref[...], rows_ref[:, tile], preferred_element_type=F32)
        out_ref[:, tile] = (first * both[:toks] + second * both[toks:]).astype(BF16)
        copies.append(
            pltpu.make_async_copy(out_ref.at[:, tile], out_hbm.at[:, tile], sems.at[part])
        )
        copies[-1].start()
    for copy in copies:
        copy.wait()


def combine(pick, gates, rows):
    toks = gates.shape[1]
    slots, width = rows.shape
    held = pl.BlockSpec(memory_space=pltpu.VMEM)
    return pl.pallas_call(
        combine_kernel,
        in_specs=[held] * 3,
        out_specs=pl.BlockSpec(memory_space=pltpu.HBM),
        out_shape=pltpu.HBM((toks, width), BF16),
        scratch_shapes=[pltpu.VMEM((toks, width), BF16), pltpu.SemaphoreType.DMA((PARTS,))],
        compiler_params=pltpu.CompilerParams(vmem_limit_bytes=16 * 2**20),
        cost_estimate=pl.CostEstimate(
            flops=4 * toks * slots * width, bytes_accessed=2 * slots * width, transcendentals=0
        ),
        name="combine",
    )(pick, gates, rows)


def add_round(value, size, flip, step):
    return value + lax.ppermute(value, AXES, [(i, i ^ flip) for i in range(size) if (i // step) % 2 == 1])


def hand_over(value, size, step, sender):
    turn = step if sender == 0 else -step
    return lax.ppermute(value, AXES, [(i, i + turn) for i in range(size) if (i // step) % 2 == sender])


def on_device(tokens, expert_ids, gate_weights, w_gate, w_up, w_down):
    toks, width = tokens.shape
    picks = expert_ids.shape[1]
    group = lax.axis_size("expert")
    copies = lax.axis_size("dp")
    experts = w_gate.shape[0] * group
    cap = min(toks * picks // 4, 3 * toks * picks // experts)
    all_tokens = toks * group * copies

    size = copies * group
    stride = 2 * group
    ids, gates = expert_ids.T, gate_weights.T
    outgoing, stats = pack(ids, gates, tokens, experts, cap)
    stats = stats + hand_over(stats, size, group, 0)
    late = lax.axis_index("dp") % 2 == 1

    def plane_sum(value):
        for flip in (1, 3, 4, 12):
            value = add_round(value, size, flip, group)
        return value

    stats = lax.cond(late, plane_sum, lambda value: value, stats)
    stats, outgoing = lax.optimization_barrier((stats, outgoing))
    received = lax.all_to_all(outgoing, "expert", split_axis=0, concat_axis=0, tiled=True)
    result = down_of(hidden_of(received, w_gate, w_up), w_down)
    stats, result, ids, gates = lax.optimization_barrier((stats, result, ids, gates))
    returned = lax.all_to_all(result, "expert", split_axis=0, concat_axis=0, tiled=True)
    pick = select(ids, experts * cap, cap)
    for flip in (1, 2, 7):
        stats = add_round(stats, size, flip * stride, group)
    stats = jnp.where(late, stats, hand_over(stats, size, group, 1))
    load, mass = stats[0, :experts], stats[1, :experts]
    aux_loss = experts * jnp.sum(load / (all_tokens * picks) * (mass / all_tokens))
    return combine(pick, gates, returned), aux_loss


def solution(mesh):
    rows = P(("dp", "expert"), None)
    held = P("expert", None, None)
    return jax.shard_map(
        on_device,
        mesh=mesh,
        in_specs=(rows, rows, rows, held, held, held),
        out_specs=(rows, P()),
        check_vma=False,
    )
```

```python
import functools

import jax
import jax.numpy as jnp
from jax import lax
from jax.experimental import pallas as pl
from jax.experimental.pallas import tpu as pltpu
from jax.sharding import PartitionSpec as P

F32 = jnp.float32
BF16 = jnp.bfloat16
PARTS = 4
AXES = ("dp", "expert")


def slots_of(ids, cap):
    toks = ids.shape[1]
    labels = lax.broadcasted_iota(jnp.int32, (toks, toks), 0)
    lanes = lax.broadcasted_iota(jnp.int32, (toks, toks), 1)
    first = (labels == ids[0:1, :]).astype(F32)
    second = (labels == ids[1:2, :]).astype(F32)
    earlier = (labels < lanes).astype(F32).astype(BF16)
    first_rank = jnp.dot(first.astype(BF16), earlier, preferred_element_type=F32)
    second_rank = jnp.dot(second.astype(BF16), earlier, preferred_element_type=F32)
    first_count = jnp.sum(first, 1, keepdims=True)
    base = ids.astype(F32) * cap
    first_slot = base[0:1, :] + jnp.sum(first * first_rank, 0, keepdims=True)
    second_slot = base[1:2, :] + jnp.sum(second * (second_rank + first_count), 0, keepdims=True)
    return first_slot, second_slot, first, second


def count_kernel(
    cap, ids_hbm, gates_hbm, tok_hbm, slot_ref, stats_ref, tok_ref, ids_ref, gates_ref, sems
):
    toks = ids_ref.shape[1]
    ids_copy = pltpu.make_async_copy(ids_hbm, ids_ref, sems.at[0])
    gates_copy = pltpu.make_async_copy(gates_hbm, gates_ref, sems.at[1])
    tok_copy = pltpu.make_async_copy(tok_hbm, tok_ref, sems.at[2])
    ids_copy.start()
    gates_copy.start()
    tok_copy.start()
    ids_copy.wait()
    first_slot, second_slot, first, second = slots_of(ids_ref[...], cap)
    slot_ref[0:1, :] = first_slot.astype(jnp.int32)
    slot_ref[1:2, :] = second_slot.astype(jnp.int32)
    count = jnp.sum(first + second, 1, keepdims=True)
    gates_copy.wait()
    gates = gates_ref[...]
    mass = jnp.sum(first * gates[0:1, :] + second * gates[1:2, :], 1, keepdims=True)
    lanes = lax.broadcasted_iota(jnp.int32, (toks, toks), 1)
    stats_ref[...] = jnp.where(lanes == 0, count, jnp.where(lanes == 1, mass, 0.0)).T[:8, :]
    tok_copy.wait()


def count(ids, gates, tokens, cap):
    toks = ids.shape[1]
    return pl.pallas_call(
        functools.partial(count_kernel, cap),
        in_specs=[pl.BlockSpec(memory_space=pltpu.HBM)] * 3,
        out_specs=[pl.BlockSpec(memory_space=pltpu.VMEM)] * 3,
        out_shape=[
            jax.ShapeDtypeStruct((8, toks), jnp.int32),
            jax.ShapeDtypeStruct((8, toks), F32),
            jax.ShapeDtypeStruct(tokens.shape, tokens.dtype),
        ],
        scratch_shapes=[
            pltpu.VMEM(ids.shape, ids.dtype),
            pltpu.VMEM(gates.shape, gates.dtype),
            pltpu.SemaphoreType.DMA((3,)),
        ],
        compiler_params=pltpu.CompilerParams(vmem_limit_bytes=4 * 2**20),
        cost_estimate=pl.CostEstimate(flops=4 * toks**3, bytes_accessed=8 * toks, transcendentals=0),
        name="count",
    )(*(pltpu.with_memory_space_constraint(a, pltpu.HBM) for a in (ids, gates, tokens)))


def pack_kernel(slot_ref, tok_ref, out_ref):
    toks = tok_ref.shape[0]
    rows = out_ref.shape[0] // PARTS
    tokens = tok_ref[...]
    first_slot, second_slot = slot_ref[0:1, :], slot_ref[1:2, :]
    for part in range(PARTS):
        slot = lax.broadcasted_iota(jnp.int32, (rows, toks), 0) + part * rows
        pick = ((slot == first_slot) | (slot == second_slot)).astype(F32).astype(BF16)
        out_ref[part * rows : (part + 1) * rows, :] = jnp.dot(
            pick, tokens, preferred_element_type=F32
        ).astype(BF16)


def pack(slots, tokens, count):
    toks, width = tokens.shape
    held = pl.BlockSpec(memory_space=pltpu.VMEM)
    return pl.pallas_call(
        pack_kernel,
        in_specs=[held] * 2,
        out_specs=held,
        out_shape=jax.ShapeDtypeStruct((count, width), BF16),
        compiler_params=pltpu.CompilerParams(vmem_limit_bytes=8 * 2**20),
        cost_estimate=pl.CostEstimate(
            flops=2 * count * toks * width, bytes_accessed=4 * count * width, transcendentals=0
        ),
        name="pack",
    )(slots, tokens)


def hidden_kernel(x_ref, gate_ref, up_ref, out_ref):
    x = x_ref[...]
    for start in range(0, out_ref.shape[1], 256):
        tile = slice(start, start + 256)
        gate = jnp.dot(x, gate_ref[0, :, tile], preferred_element_type=F32)
        up = jnp.dot(x, up_ref[0, :, tile], preferred_element_type=F32)
        out_ref[:, tile] = (gate / (1.0 + jnp.exp(-gate)) * up).astype(BF16)


def hidden_of(x, w_gate, w_up):
    rows, width = x.shape
    middle = w_gate.shape[2]
    held = pl.BlockSpec(memory_space=pltpu.VMEM)
    return pl.pallas_call(
        hidden_kernel,
        in_specs=[held] * 3,
        out_specs=held,
        out_shape=jax.ShapeDtypeStruct((rows, middle), BF16),
        compiler_params=pltpu.CompilerParams(vmem_limit_bytes=16 * 2**20),
        cost_estimate=pl.CostEstimate(
            flops=4 * rows * width * middle,
            bytes_accessed=2 * rows * width + 4 * width * middle,
            transcendentals=rows * middle,
        ),
        name="hidden",
    )(x, w_gate, w_up)


def down_kernel(x_ref, down_ref, out_hbm, out_ref, sems):
    rows = x_ref.shape[0]
    copies = []
    start = 0
    for part, size in enumerate((rows // 2, rows // 3, rows // 6)):
        tile = pl.ds(start, size)
        out_ref[tile, :] = jnp.dot(
            x_ref[tile, :], down_ref[0], preferred_element_type=F32
        ).astype(BF16)
        copies.append(pltpu.make_async_copy(out_ref.at[tile], out_hbm.at[tile], sems.at[part]))
        copies[-1].start()
        start += size
    for copy in copies:
        copy.wait()


def down_of(x, w_down):
    rows, middle = x.shape
    width = w_down.shape[2]
    held = pl.BlockSpec(memory_space=pltpu.VMEM)
    return pl.pallas_call(
        down_kernel,
        in_specs=[held] * 2,
        out_specs=pl.BlockSpec(memory_space=pltpu.HBM),
        out_shape=pltpu.HBM((rows, width), BF16),
        scratch_shapes=[pltpu.VMEM((rows, width), BF16), pltpu.SemaphoreType.DMA((3,))],
        compiler_params=pltpu.CompilerParams(vmem_limit_bytes=16 * 2**20),
        cost_estimate=pl.CostEstimate(
            flops=2 * rows * width * middle,
            bytes_accessed=2 * rows * width + 2 * width * middle,
            transcendentals=0,
        ),
        name="down",
    )(x, w_down)


def select_kernel(cap, ids_ref, pick_ref):
    toks, slots = ids_ref.shape[1], pick_ref.shape[1]
    first_slot, second_slot, _, _ = slots_of(ids_ref[...], cap)
    labels = lax.broadcasted_iota(jnp.int32, (toks, toks), 0)
    lines = jnp.where(labels == 0, first_slot, jnp.where(labels == 1, second_slot, 0.0)).T
    dest = lines[:, 0:2].astype(jnp.int32)
    lane = lax.broadcasted_iota(jnp.int32, (toks, slots), 1)
    pick_ref[:toks, :] = (lane == dest[:, 0:1]).astype(F32).astype(BF16)
    pick_ref[toks:, :] = (lane == dest[:, 1:2]).astype(F32).astype(BF16)


def select(ids, slots, cap):
    toks = ids.shape[1]
    held = pl.BlockSpec(memory_space=pltpu.VMEM)
    return pl.pallas_call(
        functools.partial(select_kernel, cap),
        in_specs=[held],
        out_specs=held,
        out_shape=jax.ShapeDtypeStruct((2 * toks, slots), BF16),
        compiler_params=pltpu.CompilerParams(vmem_limit_bytes=4 * 2**20),
        cost_estimate=pl.CostEstimate(flops=0, bytes_accessed=4 * toks * slots, transcendentals=0),
        name="select",
    )(ids)


def combine_kernel(pick_ref, gates_ref, rows_ref, out_hbm, out_ref, sems):
    toks, width = out_ref.shape
    gates = gates_ref[...]
    labels = lax.broadcasted_iota(jnp.int32, (toks, toks), 0)
    lines = jnp.where(labels == 0, gates[0:1, :], jnp.where(labels == 1, gates[1:2, :], 0.0)).T
    first, second = lines[:, 0:1], lines[:, 1:2]
    block = width // PARTS
    copies = []
    for part in range(PARTS):
        tile = pl.ds(part * block, block)
        both = jnp.dot(pick_ref[...], rows_ref[:, tile], preferred_element_type=F32)
        out_ref[:, tile] = (first * both[:toks] + second * both[toks:]).astype(BF16)
        copies.append(
            pltpu.make_async_copy(out_ref.at[:, tile], out_hbm.at[:, tile], sems.at[part])
        )
        copies[-1].start()
    for copy in copies:
        copy.wait()


def combine(pick, gates, rows):
    toks = gates.shape[1]
    slots, width = rows.shape
    held = pl.BlockSpec(memory_space=pltpu.VMEM)
    return pl.pallas_call(
        combine_kernel,
        in_specs=[held] * 3,
        out_specs=pl.BlockSpec(memory_space=pltpu.HBM),
        out_shape=pltpu.HBM((toks, width), BF16),
        scratch_shapes=[pltpu.VMEM((toks, width), BF16), pltpu.SemaphoreType.DMA((PARTS,))],
        compiler_params=pltpu.CompilerParams(vmem_limit_bytes=16 * 2**20),
        cost_estimate=pl.CostEstimate(
            flops=4 * toks * slots * width, bytes_accessed=2 * slots * width, transcendentals=0
        ),
        name="combine",
    )(pick, gates, rows)


def add_round(value, size, flip, step):
    return value + lax.ppermute(value, AXES, [(i, i ^ flip) for i in range(size) if (i // step) % 2 == 1])


def hand_over(value, size, step, sender):
    turn = step if sender == 0 else -step
    return lax.ppermute(value, AXES, [(i, i + turn) for i in range(size) if (i // step) % 2 == sender])


def on_device(tokens, expert_ids, gate_weights, w_gate, w_up, w_down):
    toks, width = tokens.shape
    picks = expert_ids.shape[1]
    group = lax.axis_size("expert")
    copies = lax.axis_size("dp")
    experts = w_gate.shape[0] * group
    cap = min(toks * picks // 4, 3 * toks * picks // experts)
    all_tokens = toks * group * copies

    size = copies * group
    stride = 2 * group
    ids, gates = expert_ids.T, gate_weights.T
    slots, stats, tokens = count(ids, gates, tokens, cap)
    swap = [(i, i + group if (i // group) % 2 == 0 else i - group) for i in range(size)]
    stats = stats + lax.ppermute(stats, AXES, swap)
    outgoing = pack(slots, tokens, experts * cap)
    late = lax.axis_index("dp") % 2 == 1

    def plane_sum(value):
        for flip in (1, 3, 4, 12):
            value = add_round(value, size, flip, group)
        return value

    stats = lax.cond(late, plane_sum, lambda value: value, stats)
    stats, outgoing = lax.optimization_barrier((stats, outgoing))
    received = lax.all_to_all(outgoing, "expert", split_axis=0, concat_axis=0, tiled=True)
    result = down_of(hidden_of(received, w_gate, w_up), w_down)
    stats, result, ids, gates = lax.optimization_barrier((stats, result, ids, gates))
    returned = lax.all_to_all(result, "expert", split_axis=0, concat_axis=0, tiled=True)
    pick = select(ids, experts * cap, cap)
    for flip in (1, 2, 7):
        stats = add_round(stats, size, flip * stride, group)
    stats = jnp.where(late, stats, hand_over(stats, size, group, 1))
    load, mass = stats[0, :experts], stats[1, :experts]
    aux_loss = experts * jnp.sum(load / (all_tokens * picks) * (mass / all_tokens))
    return combine(pick, gates, returned), aux_loss


def solution(mesh):
    rows = P(("dp", "expert"), None)
    held = P("expert", None, None)
    return jax.shard_map(
        on_device,
        mesh=mesh,
        in_specs=(rows, rows, rows, held, held, held),
        out_specs=(rows, P()),
        check_vma=False,
    )
```

```python
import functools

import jax
import jax.numpy as jnp
from jax import lax
from jax.experimental import pallas as pl
from jax.experimental.pallas import tpu as pltpu
from jax.sharding import PartitionSpec as P

F32 = jnp.float32
BF16 = jnp.bfloat16
PARTS = 4
AXES = ("dp", "expert")


def slots_of(ids, cap):
    toks = ids.shape[1]
    labels = lax.broadcasted_iota(jnp.int32, (toks, toks), 0)
    lanes = lax.broadcasted_iota(jnp.int32, (toks, toks), 1)
    first = (labels == ids[0:1, :]).astype(F32)
    second = (labels == ids[1:2, :]).astype(F32)
    earlier = (labels < lanes).astype(F32).astype(BF16)
    first_rank = jnp.dot(first.astype(BF16), earlier, preferred_element_type=F32)
    second_rank = jnp.dot(second.astype(BF16), earlier, preferred_element_type=F32)
    first_count = jnp.sum(first, 1, keepdims=True)
    base = ids.astype(F32) * cap
    first_slot = base[0:1, :] + jnp.sum(first * first_rank, 0, keepdims=True)
    second_slot = base[1:2, :] + jnp.sum(second * (second_rank + first_count), 0, keepdims=True)
    return first_slot, second_slot, first, second


def count_kernel(
    experts, cap, ids_hbm, gates_hbm, tok_hbm, slot_ref, stats_ref, tok_ref, gates_ref, ids_ref, sems
):
    toks = ids_ref.shape[1]
    ids_copy = pltpu.make_async_copy(ids_hbm, ids_ref, sems.at[0])
    gates_copy = pltpu.make_async_copy(gates_hbm, gates_ref, sems.at[1])
    tok_copy = pltpu.make_async_copy(tok_hbm, tok_ref, sems.at[2])
    ids_copy.start()
    gates_copy.start()
    tok_copy.start()
    ids_copy.wait()
    first_slot, second_slot, first, second = slots_of(ids_ref[...], cap)
    count = jnp.sum(first + second, 1, keepdims=True)
    gates_copy.wait()
    gates = gates_ref[...]
    mass = jnp.sum(first * gates[0:1, :] + second * gates[1:2, :], 1, keepdims=True)
    lanes = lax.broadcasted_iota(jnp.int32, (toks, toks), 1)
    stats = jnp.where(lanes == 0, count, jnp.where(lanes == 1, mass, 0.0)).T[:8, :]
    stats_ref[...] = stats
    lane, line = lanes[:8, :], lax.broadcasted_iota(jnp.int32, (8, toks), 0)
    free = ((stats[0:1, :] < cap) & (lane < experts)).astype(jnp.int32)
    slots = jnp.where(line == 0, first_slot.astype(jnp.int32), second_slot.astype(jnp.int32))
    slot_ref[...] = jnp.where(line < 2, slots, free)
    tok_copy.wait()


def count(ids, gates, tokens, experts, cap):
    toks = ids.shape[1]
    return pl.pallas_call(
        functools.partial(count_kernel, experts, cap),
        in_specs=[pl.BlockSpec(memory_space=pltpu.HBM)] * 3,
        out_specs=[pl.BlockSpec(memory_space=pltpu.VMEM)] * 4,
        out_shape=[
            jax.ShapeDtypeStruct((8, toks), jnp.int32),
            jax.ShapeDtypeStruct((8, toks), F32),
            jax.ShapeDtypeStruct(tokens.shape, tokens.dtype),
            jax.ShapeDtypeStruct(gates.shape, gates.dtype),
        ],
        scratch_shapes=[
            pltpu.VMEM(ids.shape, ids.dtype),
            pltpu.SemaphoreType.DMA((3,)),
        ],
        compiler_params=pltpu.CompilerParams(vmem_limit_bytes=4 * 2**20),
        cost_estimate=pl.CostEstimate(flops=4 * toks**3, bytes_accessed=8 * toks, transcendentals=0),
        name="count",
    )(*(pltpu.with_memory_space_constraint(a, pltpu.HBM) for a in (ids, gates, tokens)))


def pieces(value, count):
    parts = []
    for _ in range(count):
        parts.append(value.astype(BF16).astype(F32))
        value = value - parts[-1]
    return parts


def pack_kernel(slot_ref, tok_ref, out_ref):
    toks = tok_ref.shape[0]
    rows = out_ref.shape[0] // PARTS
    tokens = tok_ref[...]
    first_slot, second_slot = slot_ref[0:1, :], slot_ref[1:2, :]
    for part in range(PARTS):
        slot = lax.broadcasted_iota(jnp.int32, (rows, toks), 0) + part * rows
        pick = ((slot == first_slot) | (slot == second_slot)).astype(F32).astype(BF16)
        out_ref[part * rows : (part + 1) * rows, :] = jnp.dot(
            pick, tokens, preferred_element_type=F32
        ).astype(BF16)


def pack(slots, tokens, count):
    toks, width = tokens.shape
    held = pl.BlockSpec(memory_space=pltpu.VMEM)
    return pl.pallas_call(
        pack_kernel,
        in_specs=[held] * 2,
        out_specs=held,
        out_shape=jax.ShapeDtypeStruct((count, width), BF16),
        compiler_params=pltpu.CompilerParams(vmem_limit_bytes=8 * 2**20),
        cost_estimate=pl.CostEstimate(
            flops=2 * count * toks * width, bytes_accessed=4 * count * width, transcendentals=0
        ),
        name="pack",
    )(slots, tokens)


def is_free(slot_ref, expert):
    lane = lax.broadcasted_iota(jnp.int32, (1, slot_ref.shape[1]), 1)
    return jnp.sum(jnp.where(lane == expert, slot_ref[2:3, :], 0), 1, keepdims=True) > 0


def note_kernel(experts, cap, slot_ref, sums_ref, in_ref, out_ref):
    lines = pieces(sums_ref[0:1, :], 2) + pieces(sums_ref[1:2, :], 3)
    line = jnp.concatenate(lines, 1)
    edge = line.shape[1]
    line = jnp.broadcast_to(line, (16, edge))
    last = lax.broadcasted_iota(jnp.int32, (16, edge), 0) == 15
    for e in range(experts):
        tile = slice((e + 1) * cap - 16, (e + 1) * cap)
        old = in_ref[tile, :edge].astype(F32)
        out_ref[tile, :edge] = jnp.where(last & is_free(slot_ref, e), line, old).astype(BF16)


def note(slots, sums, rows, experts, cap):
    held = pl.BlockSpec(memory_space=pltpu.VMEM)
    return pl.pallas_call(
        functools.partial(note_kernel, experts, cap),
        in_specs=[held] * 3,
        out_specs=held,
        out_shape=jax.ShapeDtypeStruct(rows.shape, rows.dtype),
        input_output_aliases={2: 0},
        compiler_params=pltpu.CompilerParams(vmem_limit_bytes=4 * 2**20),
        cost_estimate=pl.CostEstimate(flops=0, bytes_accessed=2**16, transcendentals=0),
        name="note",
    )(slots, sums, rows)


def hidden_kernel(experts, cap, tokens, x_ref, gate_ref, up_ref, out_ref, loss_ref):
    lanes = loss_ref.shape[1]
    total = jnp.zeros((16, 5 * lanes), F32)
    for end in range(cap, x_ref.shape[0] + 1, cap):
        total = total + x_ref[end - 16 : end, : 5 * lanes].astype(F32)
    part = [total[15:16, i * lanes : (i + 1) * lanes] for i in range(5)]
    load, mass = part[0] + part[1], part[2] + part[3] + part[4]
    loss = experts * jnp.sum(load / (2 * tokens) * (mass / tokens), 1, keepdims=True)
    lane = lax.broadcasted_iota(jnp.int32, loss_ref.shape, 1)
    high, middle, low = pieces(loss, 3)
    line = jnp.where(lane == 0, high, jnp.where(lane == 1, middle, jnp.where(lane == 2, low, 0.0)))
    loss_ref[...] = line
    x = x_ref[...]
    for start in range(0, out_ref.shape[1], 256):
        tile = slice(start, start + 256)
        gate = jnp.dot(x, gate_ref[0, :, tile], preferred_element_type=F32)
        up = jnp.dot(x, up_ref[0, :, tile], preferred_element_type=F32)
        out_ref[:, tile] = (gate / (1.0 + jnp.exp(-gate)) * up).astype(BF16)


def hidden_of(x, w_gate, w_up, experts, cap, tokens):
    rows, width = x.shape
    middle = w_gate.shape[2]
    held = pl.BlockSpec(memory_space=pltpu.VMEM)
    return pl.pallas_call(
        functools.partial(hidden_kernel, experts, cap, tokens),
        in_specs=[held] * 3,
        out_specs=[held] * 2,
        out_shape=[jax.ShapeDtypeStruct((rows, middle), BF16), jax.ShapeDtypeStruct((8, 128), F32)],
        compiler_params=pltpu.CompilerParams(vmem_limit_bytes=16 * 2**20),
        cost_estimate=pl.CostEstimate(
            flops=4 * rows * width * middle,
            bytes_accessed=2 * rows * width + 4 * width * middle,
            transcendentals=rows * middle,
        ),
        name="hidden",
    )(x, w_gate, w_up)


def down_kernel(cap, mine_ref, slot_ref, loss_ref, x_ref, down_ref, out_ref):
    for start in range(0, x_ref.shape[0], 256):
        tile = slice(start, start + 256)
        out_ref[tile, :] = jnp.dot(
            x_ref[tile, :], down_ref[0], preferred_element_type=F32
        ).astype(BF16)
    row = lax.broadcasted_iota(jnp.int32, (16, 128), 0)
    here = (row == 15) & is_free(slot_ref, mine_ref[0])
    line = jnp.broadcast_to(loss_ref[0:1, :], (16, 128))
    for end in range(cap, x_ref.shape[0] + 1, cap):
        tile = slice(end - 16, end)
        old = out_ref[tile, 0:128].astype(F32)
        out_ref[tile, 0:128] = jnp.where(here, line, old).astype(BF16)


def down_of(mine, slots, loss, x, w_down, cap):
    rows, middle = x.shape
    width = w_down.shape[2]
    held = pl.BlockSpec(memory_space=pltpu.VMEM)
    return pl.pallas_call(
        functools.partial(down_kernel, cap),
        in_specs=[pl.BlockSpec(memory_space=pltpu.SMEM)] + [held] * 4,
        out_specs=held,
        out_shape=jax.ShapeDtypeStruct((rows, width), BF16),
        compiler_params=pltpu.CompilerParams(vmem_limit_bytes=16 * 2**20),
        cost_estimate=pl.CostEstimate(
            flops=2 * rows * width * middle,
            bytes_accessed=2 * rows * width + 2 * width * middle,
            transcendentals=0,
        ),
        name="down",
    )(mine, slots, loss, x, w_down)


def select_kernel(slot_ref, pick_ref):
    toks, slots = slot_ref.shape[1], pick_ref.shape[1]
    labels = lax.broadcasted_iota(jnp.int32, (toks, toks), 0)
    first_slot, second_slot = slot_ref[0:1, :].astype(F32), slot_ref[1:2, :].astype(F32)
    lines = jnp.where(labels == 0, first_slot, jnp.where(labels == 1, second_slot, 0.0)).T
    dest = lines[:, 0:2].astype(jnp.int32)
    lane = lax.broadcasted_iota(jnp.int32, (toks, slots), 1)
    pick_ref[:toks, :] = (lane == dest[:, 0:1]).astype(F32).astype(BF16)
    pick_ref[toks:, :] = (lane == dest[:, 1:2]).astype(F32).astype(BF16)


def select(slots, count):
    toks = slots.shape[1]
    held = pl.BlockSpec(memory_space=pltpu.VMEM)
    return pl.pallas_call(
        select_kernel,
        in_specs=[held],
        out_specs=held,
        out_shape=jax.ShapeDtypeStruct((2 * toks, count), BF16),
        compiler_params=pltpu.CompilerParams(vmem_limit_bytes=4 * 2**20),
        cost_estimate=pl.CostEstimate(flops=0, bytes_accessed=4 * toks * count, transcendentals=0),
        name="select",
    )(slots)


def read_kernel(cap, slot_ref, rows_ref, out_ref):
    line = rows_ref[3 * cap - 16 : 3 * cap, 0:128].astype(F32)[15:16, :]
    for e in (1, 0):
        other = rows_ref[(e + 1) * cap - 16 : (e + 1) * cap, 0:128].astype(F32)[15:16, :]
        line = jnp.where(is_free(slot_ref, e), other, line)
    out_ref[...] = jnp.broadcast_to(line, out_ref.shape)


def read(slots, rows, cap):
    held = pl.BlockSpec(memory_space=pltpu.VMEM)
    return pl.pallas_call(
        functools.partial(read_kernel, cap),
        in_specs=[held] * 2,
        out_specs=held,
        out_shape=jax.ShapeDtypeStruct((8, 128), F32),
        compiler_params=pltpu.CompilerParams(vmem_limit_bytes=4 * 2**20),
        cost_estimate=pl.CostEstimate(flops=0, bytes_accessed=2**14, transcendentals=0),
        name="read",
    )(slots, rows)


def loss_kernel(late_ref, mine_ref, other_ref, out_ref):
    lane = lax.broadcasted_iota(jnp.int32, (1, 128), 1)
    line = jnp.where(late_ref[0] > 0, mine_ref[0:1, :], other_ref[0:1, :])
    out_ref[0, 0] = jnp.sum(jnp.where(lane < 3, line, 0.0))


def loss_of(late, mine, other):
    held = pl.BlockSpec(memory_space=pltpu.VMEM)
    far = pl.BlockSpec(memory_space=pltpu.SMEM)
    return pl.pallas_call(
        loss_kernel,
        in_specs=[far, held, held],
        out_specs=far,
        out_shape=jax.ShapeDtypeStruct((1, 1), F32),
        compiler_params=pltpu.CompilerParams(vmem_limit_bytes=2**20),
        name="loss",
    )(late, mine, other)


def combine_kernel(pick_ref, gates_ref, rows_ref, out_hbm, out_ref, sems):
    toks, width = out_ref.shape
    gates = gates_ref[...]
    labels = lax.broadcasted_iota(jnp.int32, (toks, toks), 0)
    lines = jnp.where(labels == 0, gates[0:1, :], jnp.where(labels == 1, gates[1:2, :], 0.0)).T
    first, second = lines[:, 0:1], lines[:, 1:2]
    block = width // PARTS
    copies = []
    for part in range(PARTS):
        tile = pl.ds(part * block, block)
        both = jnp.dot(pick_ref[...], rows_ref[:, tile], preferred_element_type=F32)
        out_ref[:, tile] = (first * both[:toks] + second * both[toks:]).astype(BF16)
        copies.append(
            pltpu.make_async_copy(out_ref.at[:, tile], out_hbm.at[:, tile], sems.at[part])
        )
        copies[-1].start()
    for copy in copies:
        copy.wait()


def combine(pick, gates, rows):
    toks = gates.shape[1]
    slots, width = rows.shape
    held = pl.BlockSpec(memory_space=pltpu.VMEM)
    return pl.pallas_call(
        combine_kernel,
        in_specs=[held] * 3,
        out_specs=pl.BlockSpec(memory_space=pltpu.HBM),
        out_shape=pltpu.HBM((toks, width), BF16),
        scratch_shapes=[pltpu.VMEM((toks, width), BF16), pltpu.SemaphoreType.DMA((PARTS,))],
        compiler_params=pltpu.CompilerParams(vmem_limit_bytes=16 * 2**20),
        cost_estimate=pl.CostEstimate(
            flops=4 * toks * slots * width, bytes_accessed=2 * slots * width, transcendentals=0
        ),
        name="combine",
    )(pick, gates, rows)


def add_round(value, size, flip, step):
    return value + lax.ppermute(value, AXES, [(i, i ^ flip) for i in range(size) if (i // step) % 2 == 1])


def on_device(tokens, expert_ids, gate_weights, w_gate, w_up, w_down):
    toks, width = tokens.shape
    picks = expert_ids.shape[1]
    group = lax.axis_size("expert")
    copies = lax.axis_size("dp")
    experts = w_gate.shape[0] * group
    cap = min(toks * picks // 4, 3 * toks * picks // experts)
    all_tokens = toks * group * copies

    size = copies * group
    stride = 2 * group
    ids, gates = expert_ids.T, gate_weights.T
    slots, stats, tokens, gates = count(ids, gates, tokens, experts, cap)
    swap = [(i, i + group if (i // group) % 2 == 0 else i - group) for i in range(size)]
    late = lax.axis_index("dp") % 2
    mine = lax.axis_index("expert").reshape(1)
    other = lax.ppermute(stats, AXES, swap)
    outgoing = pack(slots, tokens, experts * cap)
    pick = select(slots, experts * cap)

    def column_sum(value, other):
        value = value + other
        for flip in (1, 2, 7):
            value = add_round(value, size, flip * stride, group)
        return value

    stats = lax.cond(late == 1, column_sum, lambda value, other: value, stats, other)
    outgoing = note(slots, stats, outgoing, experts, cap)
    late, mine, pick, outgoing = lax.optimization_barrier((late.reshape(1), mine, pick, outgoing))
    received = lax.all_to_all(outgoing, "expert", split_axis=0, concat_axis=0, tiled=True)
    hidden, loss = hidden_of(received, w_gate, w_up, experts, cap, all_tokens)
    result = down_of(mine, slots, loss, hidden, w_down, cap)
    returned = lax.all_to_all(result, "expert", split_axis=0, concat_axis=0, tiled=True)
    loss = read(slots, returned, cap)
    other = lax.ppermute(loss, AXES, swap)
    mixed = combine(pick, gates, returned)
    other, mixed = lax.optimization_barrier((other, mixed))
    return mixed, loss_of(late, loss, other).reshape(())


def solution(mesh):
    rows = P(("dp", "expert"), None)
    held = P("expert", None, None)
    return jax.shard_map(
        on_device,
        mesh=mesh,
        in_specs=(rows, rows, rows, held, held, held),
        out_specs=(rows, P()),
        check_vma=False,
    )
```

```python
import functools

import jax
import jax.numpy as jnp
from jax import lax
from jax.experimental import pallas as pl
from jax.experimental.pallas import tpu as pltpu
from jax.sharding import PartitionSpec as P

F32 = jnp.float32
BF16 = jnp.bfloat16
PARTS = 4
ROUNDS = (
    (1, 0, 3, 2, 5, 4, 7, 6),
    (2, 3, 0, 1, 6, 7, 4, 5),
    (6, 7, 4, 5, 2, 3, 0, 1),
)
AXES = ("dp", "expert")


def slots_of(ids, experts, cap):
    toks = ids.shape[1]
    labels = lax.broadcasted_iota(jnp.int32, (experts, toks), 0)
    first = (labels == ids[0:1, :]).astype(F32)
    second = (labels == ids[1:2, :]).astype(F32)
    before = lax.broadcasted_iota(jnp.int32, (toks, toks), 0)
    earlier = (before < lax.broadcasted_iota(jnp.int32, (toks, toks), 1)).astype(F32).astype(BF16)
    both = jnp.concatenate([first, second], 0).astype(BF16)
    rank = jnp.dot(both, earlier, preferred_element_type=F32)
    first_rank, second_rank = rank[:experts], rank[experts:]
    first_count = jnp.sum(first, 1, keepdims=True)
    base = ids.astype(F32) * cap
    first_slot = base[0:1, :] + jnp.sum(first * first_rank, 0, keepdims=True)
    second_slot = base[1:2, :] + jnp.sum(second * (second_rank + first_count), 0, keepdims=True)
    return first_slot, second_slot, first, second


def count_kernel(
    experts, cap, ids_hbm, gates_hbm, tok_hbm, slot_ref, stats_ref, tok_ref, gates_ref, ids_ref, sems
):
    toks = ids_ref.shape[1]
    ids_copy = pltpu.make_async_copy(ids_hbm, ids_ref, sems.at[0])
    gates_copy = pltpu.make_async_copy(gates_hbm, gates_ref, sems.at[1])
    tok_copy = pltpu.make_async_copy(tok_hbm, tok_ref, sems.at[2])
    ids_copy.start()
    gates_copy.start()
    tok_copy.start()
    ids_copy.wait()
    first_slot, second_slot, first, second = slots_of(ids_ref[...], experts, cap)
    count = jnp.sum(first + second, 1, keepdims=True)
    gates_copy.wait()
    gates = gates_ref[...]
    mass = jnp.sum(first * gates[0:1, :] + second * gates[1:2, :], 1, keepdims=True)
    lanes = lax.broadcasted_iota(jnp.int32, (experts, toks), 1)
    stats = jnp.where(lanes == 0, count, jnp.where(lanes == 1, mass, 0.0))
    stats = jnp.concatenate([stats, jnp.zeros((toks - experts, toks), F32)], 0).T[:8, :]
    stats_ref[...] = stats
    lane = lax.broadcasted_iota(jnp.int32, (8, toks), 1)
    line = lax.broadcasted_iota(jnp.int32, (8, toks), 0)
    free = ((stats[0:1, :] < cap) & (lane < experts)).astype(jnp.int32)
    slots = jnp.where(line == 0, first_slot.astype(jnp.int32), second_slot.astype(jnp.int32))
    slot_ref[...] = jnp.where(line < 2, slots, free)
    tok_copy.wait()


def count(ids, gates, tokens, experts, cap):
    toks = ids.shape[1]
    return pl.pallas_call(
        functools.partial(count_kernel, experts, cap),
        in_specs=[pl.BlockSpec(memory_space=pltpu.HBM)] * 3,
        out_specs=[pl.BlockSpec(memory_space=pltpu.VMEM)] * 4,
        out_shape=[
            jax.ShapeDtypeStruct((8, toks), jnp.int32),
            jax.ShapeDtypeStruct((8, toks), F32),
            jax.ShapeDtypeStruct(tokens.shape, tokens.dtype),
            jax.ShapeDtypeStruct(gates.shape, gates.dtype),
        ],
        scratch_shapes=[
            pltpu.VMEM(ids.shape, ids.dtype),
            pltpu.SemaphoreType.DMA((3,)),
        ],
        compiler_params=pltpu.CompilerParams(vmem_limit_bytes=4 * 2**20),
        cost_estimate=pl.CostEstimate(flops=4 * toks**3, bytes_accessed=8 * toks, transcendentals=0),
        name="count",
    )(*(pltpu.with_memory_space_constraint(a, pltpu.HBM) for a in (ids, gates, tokens)))


def pieces(value, count):
    parts = []
    for _ in range(count):
        parts.append(value.astype(BF16).astype(F32))
        value = value - parts[-1]
    return parts


def pack_kernel(slot_ref, tok_ref, out_ref):
    toks = tok_ref.shape[0]
    rows = out_ref.shape[0] // PARTS
    tokens = tok_ref[...]
    first_slot, second_slot = slot_ref[0:1, :], slot_ref[1:2, :]
    for part in range(PARTS):
        slot = lax.broadcasted_iota(jnp.int32, (rows, toks), 0) + part * rows
        pick = ((slot == first_slot) | (slot == second_slot)).astype(F32).astype(BF16)
        out_ref[part * rows : (part + 1) * rows, :] = jnp.dot(
            pick, tokens, preferred_element_type=F32
        ).astype(BF16)


def pack(slots, tokens, count):
    toks, width = tokens.shape
    held = pl.BlockSpec(memory_space=pltpu.VMEM)
    return pl.pallas_call(
        pack_kernel,
        in_specs=[held] * 2,
        out_specs=held,
        out_shape=jax.ShapeDtypeStruct((count, width), BF16),
        compiler_params=pltpu.CompilerParams(vmem_limit_bytes=8 * 2**20),
        cost_estimate=pl.CostEstimate(
            flops=2 * count * toks * width, bytes_accessed=4 * count * width, transcendentals=0
        ),
        name="pack",
    )(slots, tokens)


def is_free(slot_ref, expert):
    lane = lax.broadcasted_iota(jnp.int32, (1, slot_ref.shape[1]), 1)
    return jnp.sum(jnp.where(lane == expert, slot_ref[2:3, :], 0), 1, keepdims=True) > 0


def note_kernel(experts, cap, slot_ref, sums_ref, in_ref, out_ref):
    lines = pieces(sums_ref[0:1, :], 2) + pieces(sums_ref[1:2, :], 3)
    line = jnp.concatenate(lines, 1)
    edge = line.shape[1]
    line = jnp.broadcast_to(line, (16, edge))
    last = lax.broadcasted_iota(jnp.int32, (16, edge), 0) == 15
    for e in range(experts):
        tile = slice((e + 1) * cap - 16, (e + 1) * cap)
        old = in_ref[tile, :edge].astype(F32)
        out_ref[tile, :edge] = jnp.where(last & is_free(slot_ref, e), line, old).astype(BF16)


def note(slots, sums, rows, experts, cap):
    held = pl.BlockSpec(memory_space=pltpu.VMEM)
    return pl.pallas_call(
        functools.partial(note_kernel, experts, cap),
        in_specs=[held] * 3,
        out_specs=held,
        out_shape=jax.ShapeDtypeStruct(rows.shape, rows.dtype),
        input_output_aliases={2: 0},
        compiler_params=pltpu.CompilerParams(vmem_limit_bytes=4 * 2**20),
        cost_estimate=pl.CostEstimate(flops=0, bytes_accessed=2**16, transcendentals=0),
        name="note",
    )(slots, sums, rows)


def hidden_kernel(experts, cap, tokens, x_ref, gate_ref, up_ref, out_ref, loss_ref):
    lanes = loss_ref.shape[1]
    total = jnp.zeros((16, 5 * lanes), F32)
    for end in range(cap, x_ref.shape[0] + 1, cap):
        total = total + x_ref[end - 16 : end, : 5 * lanes].astype(F32)
    part = [total[15:16, i * lanes : (i + 1) * lanes] for i in range(5)]
    load, mass = part[0] + part[1], part[2] + part[3] + part[4]
    loss = experts * jnp.sum(load / (2 * tokens) * (mass / tokens), 1, keepdims=True)
    lane = lax.broadcasted_iota(jnp.int32, loss_ref.shape, 1)
    high, middle, low = pieces(loss, 3)
    line = jnp.where(lane == 0, high, jnp.where(lane == 1, middle, jnp.where(lane == 2, low, 0.0)))
    loss_ref[...] = line
    x = x_ref[...]
    for start in range(0, out_ref.shape[1], 256):
        tile = slice(start, start + 256)
        gate = jnp.dot(x, gate_ref[0, :, tile], preferred_element_type=F32)
        up = jnp.dot(x, up_ref[0, :, tile], preferred_element_type=F32)
        out_ref[:, tile] = (gate / (1.0 + jnp.exp(-gate)) * up).astype(BF16)


def hidden_of(x, w_gate, w_up, experts, cap, tokens):
    rows, width = x.shape
    middle = w_gate.shape[2]
    held = pl.BlockSpec(memory_space=pltpu.VMEM)
    return pl.pallas_call(
        functools.partial(hidden_kernel, experts, cap, tokens),
        in_specs=[held] * 3,
        out_specs=[held] * 2,
        out_shape=[jax.ShapeDtypeStruct((rows, middle), BF16), jax.ShapeDtypeStruct((8, 128), F32)],
        compiler_params=pltpu.CompilerParams(vmem_limit_bytes=16 * 2**20),
        cost_estimate=pl.CostEstimate(
            flops=4 * rows * width * middle,
            bytes_accessed=2 * rows * width + 4 * width * middle,
            transcendentals=rows * middle,
        ),
        name="hidden",
    )(x, w_gate, w_up)


def down_kernel(cap, slot_ref, loss_ref, x_ref, down_ref, out_ref):
    for start in range(0, x_ref.shape[0], 256):
        tile = slice(start, start + 256)
        out_ref[tile, :] = jnp.dot(
            x_ref[tile, :], down_ref[0], preferred_element_type=F32
        ).astype(BF16)
    row = lax.broadcasted_iota(jnp.int32, (16, 128), 0)
    here = (row == 15) & is_free(slot_ref, lax.axis_index("expert"))
    line = jnp.broadcast_to(loss_ref[0:1, :], (16, 128))
    for end in range(cap, x_ref.shape[0] + 1, cap):
        tile = slice(end - 16, end)
        old = out_ref[tile, 0:128].astype(F32)
        out_ref[tile, 0:128] = jnp.where(here, line, old).astype(BF16)


def down_of(slots, loss, x, w_down, cap):
    rows, middle = x.shape
    width = w_down.shape[2]
    held = pl.BlockSpec(memory_space=pltpu.VMEM)
    return pl.pallas_call(
        functools.partial(down_kernel, cap),
        in_specs=[held] * 4,
        out_specs=held,
        out_shape=jax.ShapeDtypeStruct((rows, width), BF16),
        compiler_params=pltpu.CompilerParams(vmem_limit_bytes=16 * 2**20),
        cost_estimate=pl.CostEstimate(
            flops=2 * rows * width * middle,
            bytes_accessed=2 * rows * width + 2 * width * middle,
            transcendentals=0,
        ),
        name="down",
    )(slots, loss, x, w_down)


def select_kernel(slot_ref, pick_ref):
    toks, slots = slot_ref.shape[1], pick_ref.shape[1]
    labels = lax.broadcasted_iota(jnp.int32, (toks, toks), 0)
    first_slot, second_slot = slot_ref[0:1, :].astype(F32), slot_ref[1:2, :].astype(F32)
    lines = jnp.where(labels == 0, first_slot, jnp.where(labels == 1, second_slot, 0.0)).T
    dest = lines[:, 0:2].astype(jnp.int32)
    lane = lax.broadcasted_iota(jnp.int32, (toks, slots), 1)
    pick_ref[:toks, :] = (lane == dest[:, 0:1]).astype(F32).astype(BF16)
    pick_ref[toks:, :] = (lane == dest[:, 1:2]).astype(F32).astype(BF16)


def select(slots, count):
    toks = slots.shape[1]
    held = pl.BlockSpec(memory_space=pltpu.VMEM)
    return pl.pallas_call(
        select_kernel,
        in_specs=[held],
        out_specs=held,
        out_shape=jax.ShapeDtypeStruct((2 * toks, count), BF16),
        compiler_params=pltpu.CompilerParams(vmem_limit_bytes=4 * 2**20),
        cost_estimate=pl.CostEstimate(flops=0, bytes_accessed=4 * toks * count, transcendentals=0),
        name="select",
    )(slots)


def read_kernel(cap, slot_ref, rows_ref, out_ref):
    line = rows_ref[3 * cap - 16 : 3 * cap, 0:128].astype(F32)[15:16, :]
    for e in (1, 0):
        other = rows_ref[(e + 1) * cap - 16 : (e + 1) * cap, 0:128].astype(F32)[15:16, :]
        line = jnp.where(is_free(slot_ref, e), other, line)
    out_ref[...] = jnp.broadcast_to(line, out_ref.shape)


def read(slots, rows, cap):
    held = pl.BlockSpec(memory_space=pltpu.VMEM)
    return pl.pallas_call(
        functools.partial(read_kernel, cap),
        in_specs=[held] * 2,
        out_specs=held,
        out_shape=jax.ShapeDtypeStruct((8, 128), F32),
        compiler_params=pltpu.CompilerParams(vmem_limit_bytes=4 * 2**20),
        cost_estimate=pl.CostEstimate(flops=0, bytes_accessed=2**14, transcendentals=0),
        name="read",
    )(slots, rows)


def loss_kernel(mine_ref, other_ref, out_ref):
    lane = lax.broadcasted_iota(jnp.int32, (1, 128), 1)
    late = lax.axis_index("dp") % 2 == 1
    line = jnp.where(late, mine_ref[0:1, :], other_ref[0:1, :])
    out_ref[0, 0] = jnp.sum(jnp.where(lane < 3, line, 0.0))


def loss_of(mine, other):
    held = pl.BlockSpec(memory_space=pltpu.VMEM)
    far = pl.BlockSpec(memory_space=pltpu.SMEM)
    return pl.pallas_call(
        loss_kernel,
        in_specs=[held] * 2,
        out_specs=far,
        out_shape=jax.ShapeDtypeStruct((1, 1), F32),
        compiler_params=pltpu.CompilerParams(vmem_limit_bytes=2**20),
        name="loss",
    )(mine, other)


def combine_kernel(pick_ref, gates_ref, rows_ref, out_hbm, out_ref, sems):
    toks, width = out_ref.shape
    gates = gates_ref[...]
    labels = lax.broadcasted_iota(jnp.int32, (toks, toks), 0)
    lines = jnp.where(labels == 0, gates[0:1, :], jnp.where(labels == 1, gates[1:2, :], 0.0)).T
    first, second = lines[:, 0:1], lines[:, 1:2]
    block = width // PARTS
    copies = []
    for part in range(PARTS):
        tile = pl.ds(part * block, block)
        both = jnp.dot(pick_ref[...], rows_ref[:, tile], preferred_element_type=F32)
        out_ref[:, tile] = (first * both[:toks] + second * both[toks:]).astype(BF16)
        copies.append(
            pltpu.make_async_copy(out_ref.at[:, tile], out_hbm.at[:, tile], sems.at[part])
        )
        copies[-1].start()
    for copy in copies:
        copy.wait()


def combine(pick, gates, rows):
    toks = gates.shape[1]
    slots, width = rows.shape
    held = pl.BlockSpec(memory_space=pltpu.VMEM)
    return pl.pallas_call(
        combine_kernel,
        in_specs=[held] * 3,
        out_specs=pl.BlockSpec(memory_space=pltpu.HBM),
        out_shape=pltpu.HBM((toks, width), BF16),
        scratch_shapes=[pltpu.VMEM((toks, width), BF16), pltpu.SemaphoreType.DMA((PARTS,))],
        compiler_params=pltpu.CompilerParams(vmem_limit_bytes=16 * 2**20),
        cost_estimate=pl.CostEstimate(
            flops=4 * toks * slots * width, bytes_accessed=2 * slots * width, transcendentals=0
        ),
        name="combine",
    )(pick, gates, rows)


def add_round(value, size, step, partner):
    stride = 2 * step
    pairs = [
        (i, partner[i // stride] * stride + i % stride) for i in range(size) if (i // step) % 2 == 1
    ]
    return value + lax.ppermute(value, AXES, pairs)


def on_device(tokens, expert_ids, gate_weights, w_gate, w_up, w_down):
    toks, width = tokens.shape
    picks = expert_ids.shape[1]
    group = lax.axis_size("expert")
    copies = lax.axis_size("dp")
    experts = w_gate.shape[0] * group
    cap = min(toks * picks // 4, 3 * toks * picks // experts)
    all_tokens = toks * group * copies

    size = copies * group
    ids, gates = expert_ids.T, gate_weights.T
    slots, stats, tokens, gates = count(ids, gates, tokens, experts, cap)
    swap = [(i, i + group if (i // group) % 2 == 0 else i - group) for i in range(size)]
    late = lax.axis_index("dp") % 2
    other = lax.ppermute(stats, AXES, swap)
    outgoing = pack(slots, tokens, experts * cap)
    pick = select(slots, experts * cap)

    def column_sum(value, other):
        value = value + other
        for partner in ROUNDS:
            value = add_round(value, size, group, partner)
        return value

    stats = lax.cond(late == 1, column_sum, lambda value, other: value, stats, other)
    outgoing = note(slots, stats, outgoing, experts, cap)
    pick, outgoing = lax.optimization_barrier((pick, outgoing))
    received = lax.all_to_all(outgoing, "expert", split_axis=0, concat_axis=0, tiled=True)
    hidden, loss = hidden_of(received, w_gate, w_up, experts, cap, all_tokens)
    result = down_of(slots, loss, hidden, w_down, cap)
    returned = lax.all_to_all(result, "expert", split_axis=0, concat_axis=0, tiled=True)
    loss = read(slots, returned, cap)
    other = lax.ppermute(loss, AXES, swap)
    mixed = combine(pick, gates, returned)
    other, mixed = lax.optimization_barrier((other, mixed))
    return mixed, loss_of(loss, other).reshape(())


def solution(mesh):
    rows = P(("dp", "expert"), None)
    held = P("expert", None, None)
    return jax.shard_map(
        on_device,
        mesh=mesh,
        in_specs=(rows, rows, rows, held, held, held),
        out_specs=(rows, P()),
        check_vma=False,
    )
```

```python
import functools

import jax
import jax.numpy as jnp
from jax import lax
from jax.experimental import pallas as pl
from jax.experimental.pallas import tpu as pltpu
from jax.sharding import PartitionSpec as P

F32 = jnp.float32
BF16 = jnp.bfloat16
PARTS = 4
ROUNDS = (
    (1, 0, 3, 2, 5, 4, 7, 6),
    (2, 3, 0, 1, 6, 7, 4, 5),
    (6, 7, 4, 5, 2, 3, 0, 1),
)
AXES = ("dp", "expert")


def slots_of(ids, experts, cap):
    toks = ids.shape[1]
    labels = lax.broadcasted_iota(jnp.int32, (experts, toks), 0)
    first = (labels == ids[0:1, :]).astype(F32)
    second = (labels == ids[1:2, :]).astype(F32)
    before = lax.broadcasted_iota(jnp.int32, (toks, toks), 0)
    earlier = (before < lax.broadcasted_iota(jnp.int32, (toks, toks), 1)).astype(F32).astype(BF16)
    both = jnp.concatenate([first, second], 0).astype(BF16)
    rank = jnp.dot(both, earlier, preferred_element_type=F32)
    first_rank, second_rank = rank[:experts], rank[experts:]
    first_count = jnp.sum(first, 1, keepdims=True)
    base = ids.astype(F32) * cap
    first_slot = base[0:1, :] + jnp.sum(first * first_rank, 0, keepdims=True)
    second_slot = base[1:2, :] + jnp.sum(second * (second_rank + first_count), 0, keepdims=True)
    return first_slot, second_slot, first, second


def count_kernel(
    experts, cap, ids_hbm, gates_hbm, tok_hbm, slot_ref, stats_ref, tok_ref, gates_ref, ids_ref, sems
):
    toks = ids_ref.shape[1]
    ids_copy = pltpu.make_async_copy(ids_hbm, ids_ref, sems.at[0])
    gates_copy = pltpu.make_async_copy(gates_hbm, gates_ref, sems.at[1])
    tok_copy = pltpu.make_async_copy(tok_hbm, tok_ref, sems.at[2])
    ids_copy.start()
    gates_copy.start()
    tok_copy.start()
    ids_copy.wait()
    first_slot, second_slot, first, second = slots_of(ids_ref[...], experts, cap)
    count = jnp.sum(first + second, 1, keepdims=True)
    gates_copy.wait()
    gates = gates_ref[...]
    mass = jnp.sum(first * gates[0:1, :] + second * gates[1:2, :], 1, keepdims=True)
    lanes = lax.broadcasted_iota(jnp.int32, (experts, toks), 1)
    stats = jnp.where(lanes == 0, count, jnp.where(lanes == 1, mass, 0.0))
    stats = jnp.concatenate([stats, jnp.zeros((toks - experts, toks), F32)], 0).T[:8, :]
    stats_ref[...] = stats
    lane = lax.broadcasted_iota(jnp.int32, (8, toks), 1)
    line = lax.broadcasted_iota(jnp.int32, (8, toks), 0)
    free = ((stats[0:1, :] < cap) & (lane < experts)).astype(jnp.int32)
    slots = jnp.where(line == 0, first_slot.astype(jnp.int32), second_slot.astype(jnp.int32))
    slot_ref[...] = jnp.where(line < 2, slots, free)
    tok_copy.wait()


def count(ids, gates, tokens, experts, cap):
    toks = ids.shape[1]
    return pl.pallas_call(
        functools.partial(count_kernel, experts, cap),
        in_specs=[pl.BlockSpec(memory_space=pltpu.HBM)] * 3,
        out_specs=[pl.BlockSpec(memory_space=pltpu.VMEM)] * 4,
        out_shape=[
            jax.ShapeDtypeStruct((8, toks), jnp.int32),
            jax.ShapeDtypeStruct((8, toks), F32),
            jax.ShapeDtypeStruct(tokens.shape, tokens.dtype),
            jax.ShapeDtypeStruct(gates.shape, gates.dtype),
        ],
        scratch_shapes=[
            pltpu.VMEM(ids.shape, ids.dtype),
            pltpu.SemaphoreType.DMA((3,)),
        ],
        compiler_params=pltpu.CompilerParams(vmem_limit_bytes=4 * 2**20),
        cost_estimate=pl.CostEstimate(flops=4 * toks**3, bytes_accessed=8 * toks, transcendentals=0),
        name="count",
    )(*(pltpu.with_memory_space_constraint(a, pltpu.HBM) for a in (ids, gates, tokens)))


def pieces(value, count):
    parts = []
    for _ in range(count):
        parts.append(value.astype(BF16).astype(F32))
        value = value - parts[-1]
    return parts


def pack_kernel(slot_ref, tok_ref, out_ref):
    toks = tok_ref.shape[0]
    rows = out_ref.shape[0] // PARTS
    tokens = tok_ref[...]
    first_slot, second_slot = slot_ref[0:1, :], slot_ref[1:2, :]
    for part in range(PARTS):
        slot = lax.broadcasted_iota(jnp.int32, (rows, toks), 0) + part * rows
        pick = ((slot == first_slot) | (slot == second_slot)).astype(F32).astype(BF16)
        out_ref[part * rows : (part + 1) * rows, :] = jnp.dot(
            pick, tokens, preferred_element_type=F32
        ).astype(BF16)


def pack(slots, tokens, count):
    toks, width = tokens.shape
    held = pl.BlockSpec(memory_space=pltpu.VMEM)
    return pl.pallas_call(
        pack_kernel,
        in_specs=[held] * 2,
        out_specs=held,
        out_shape=jax.ShapeDtypeStruct((count, width), BF16),
        compiler_params=pltpu.CompilerParams(vmem_limit_bytes=8 * 2**20),
        cost_estimate=pl.CostEstimate(
            flops=2 * count * toks * width, bytes_accessed=4 * count * width, transcendentals=0
        ),
        name="pack",
    )(slots, tokens)


def is_free(slot_ref, expert):
    lane = lax.broadcasted_iota(jnp.int32, (1, slot_ref.shape[1]), 1)
    return jnp.sum(jnp.where(lane == expert, slot_ref[2:3, :], 0), 1, keepdims=True) > 0


def note_kernel(experts, cap, slot_ref, sums_ref, in_ref, out_ref):
    lines = pieces(sums_ref[0:1, :], 2) + pieces(sums_ref[1:2, :], 3)
    line = jnp.concatenate(lines, 1)
    edge = line.shape[1]
    line = jnp.broadcast_to(line, (16, edge))
    last = lax.broadcasted_iota(jnp.int32, (16, edge), 0) == 15
    for e in range(experts):
        tile = slice((e + 1) * cap - 16, (e + 1) * cap)
        old = in_ref[tile, :edge].astype(F32)
        out_ref[tile, :edge] = jnp.where(last & is_free(slot_ref, e), line, old).astype(BF16)


def note(slots, sums, rows, experts, cap):
    held = pl.BlockSpec(memory_space=pltpu.VMEM)
    return pl.pallas_call(
        functools.partial(note_kernel, experts, cap),
        in_specs=[held] * 3,
        out_specs=held,
        out_shape=jax.ShapeDtypeStruct(rows.shape, rows.dtype),
        input_output_aliases={2: 0},
        compiler_params=pltpu.CompilerParams(vmem_limit_bytes=4 * 2**20),
        cost_estimate=pl.CostEstimate(flops=0, bytes_accessed=2**16, transcendentals=0),
        name="note",
    )(slots, sums, rows)


def hidden_kernel(experts, cap, tokens, slot_ref, x_ref, gate_ref, up_ref, out_ref, loss_ref, few_ref):
    lanes = loss_ref.shape[1]
    total = jnp.zeros((16, 5 * lanes), F32)
    for end in range(cap, x_ref.shape[0] + 1, cap):
        total = total + x_ref[end - 16 : end, : 5 * lanes].astype(F32)
    part = [total[15:16, i * lanes : (i + 1) * lanes] for i in range(5)]
    load, mass = part[0] + part[1], part[2] + part[3] + part[4]
    loss = experts * jnp.sum(load / (2 * tokens) * (mass / tokens), 1, keepdims=True)
    lane = lax.broadcasted_iota(jnp.int32, loss_ref.shape, 1)
    high, middle, low = pieces(loss, 3)
    line = jnp.where(lane == 0, high, jnp.where(lane == 1, middle, jnp.where(lane == 2, low, 0.0)))
    loss_ref[...] = line

    def run(rows_ref):
        rows = rows_ref.shape[0]
        x = rows_ref[...]
        for start in range(0, out_ref.shape[1], 256):
            tile = slice(start, start + 256)
            gate = jnp.dot(x, gate_ref[0, :, tile], preferred_element_type=F32)
            up = jnp.dot(x, up_ref[0, :, tile], preferred_element_type=F32)
            out_ref[:rows, tile] = (gate / (1.0 + jnp.exp(-gate)) * up).astype(BF16)

    free = mine_free(slot_ref)

    @pl.when(free)
    def _():
        for chunk in range(x_ref.shape[0] // cap):
            few_ref[chunk * 16 : chunk * 16 + 16, :] = x_ref[chunk * cap : chunk * cap + 16, :]
        run(few_ref)

    @pl.when(jnp.logical_not(free))
    def _():
        run(x_ref)


def mine_free(slot_ref):
    lane = lax.broadcasted_iota(jnp.int32, (1, slot_ref.shape[1]), 1)
    return jnp.sum(jnp.where(lane == lax.axis_index("expert"), slot_ref[2:3, :], 0)) > 0


def hidden_of(slots, x, w_gate, w_up, experts, cap, tokens):
    rows, width = x.shape
    middle = w_gate.shape[2]
    held = pl.BlockSpec(memory_space=pltpu.VMEM)
    return pl.pallas_call(
        functools.partial(hidden_kernel, experts, cap, tokens),
        in_specs=[held] * 4,
        out_specs=[held] * 2,
        out_shape=[jax.ShapeDtypeStruct((rows, middle), BF16), jax.ShapeDtypeStruct((8, 128), F32)],
        scratch_shapes=[pltpu.VMEM((rows // cap * 16, width), BF16)],
        compiler_params=pltpu.CompilerParams(vmem_limit_bytes=16 * 2**20),
        cost_estimate=pl.CostEstimate(
            flops=4 * rows * width * middle,
            bytes_accessed=2 * rows * width + 4 * width * middle,
            transcendentals=rows * middle,
        ),
        name="hidden",
    )(slots, x, w_gate, w_up)


def down_kernel(cap, slot_ref, loss_ref, x_ref, down_ref, out_ref):
    chunks = x_ref.shape[0] // cap
    free = mine_free(slot_ref)

    @pl.when(free)
    def _():
        few = chunks * 16
        rows = jnp.dot(x_ref[:few, :], down_ref[0], preferred_element_type=F32).astype(BF16)
        rest = jnp.zeros((cap - 16, out_ref.shape[1]), BF16)
        last = lax.broadcasted_iota(jnp.int32, (16, 128), 0) == 15
        line = jnp.broadcast_to(loss_ref[0:1, :], (16, 128))
        line = jnp.where(last, line, 0.0).astype(BF16)
        for chunk in range(chunks):
            start = chunk * cap
            out_ref[start : start + 16, :] = rows[chunk * 16 : chunk * 16 + 16, :]
            out_ref[start + 16 : start + cap, :] = rest
            out_ref[start + cap - 16 : start + cap, 0:128] = line

    @pl.when(jnp.logical_not(free))
    def _():
        for start in range(0, x_ref.shape[0], 256):
            tile = slice(start, start + 256)
            out_ref[tile, :] = jnp.dot(
                x_ref[tile, :], down_ref[0], preferred_element_type=F32
            ).astype(BF16)


def down_of(slots, loss, x, w_down, cap):
    rows, middle = x.shape
    width = w_down.shape[2]
    held = pl.BlockSpec(memory_space=pltpu.VMEM)
    return pl.pallas_call(
        functools.partial(down_kernel, cap),
        in_specs=[held] * 4,
        out_specs=held,
        out_shape=jax.ShapeDtypeStruct((rows, width), BF16),
        compiler_params=pltpu.CompilerParams(vmem_limit_bytes=16 * 2**20),
        cost_estimate=pl.CostEstimate(
            flops=2 * rows * width * middle,
            bytes_accessed=2 * rows * width + 2 * width * middle,
            transcendentals=0,
        ),
        name="down",
    )(slots, loss, x, w_down)


def select_kernel(slot_ref, pick_ref):
    toks, slots = slot_ref.shape[1], pick_ref.shape[1]
    labels = lax.broadcasted_iota(jnp.int32, (toks, toks), 0)
    first_slot, second_slot = slot_ref[0:1, :].astype(F32), slot_ref[1:2, :].astype(F32)
    lines = jnp.where(labels == 0, first_slot, jnp.where(labels == 1, second_slot, 0.0)).T
    dest = lines[:, 0:2].astype(jnp.int32)
    lane = lax.broadcasted_iota(jnp.int32, (toks, slots), 1)
    pick_ref[:toks, :] = (lane == dest[:, 0:1]).astype(F32).astype(BF16)
    pick_ref[toks:, :] = (lane == dest[:, 1:2]).astype(F32).astype(BF16)


def select(slots, count):
    toks = slots.shape[1]
    held = pl.BlockSpec(memory_space=pltpu.VMEM)
    return pl.pallas_call(
        select_kernel,
        in_specs=[held],
        out_specs=held,
        out_shape=jax.ShapeDtypeStruct((2 * toks, count), BF16),
        compiler_params=pltpu.CompilerParams(vmem_limit_bytes=4 * 2**20),
        cost_estimate=pl.CostEstimate(flops=0, bytes_accessed=4 * toks * count, transcendentals=0),
        name="select",
    )(slots)


def read_kernel(cap, slot_ref, rows_ref, out_ref):
    line = rows_ref[3 * cap - 16 : 3 * cap, 0:128].astype(F32)[15:16, :]
    for e in (1, 0):
        other = rows_ref[(e + 1) * cap - 16 : (e + 1) * cap, 0:128].astype(F32)[15:16, :]
        line = jnp.where(is_free(slot_ref, e), other, line)
    out_ref[...] = jnp.broadcast_to(line, out_ref.shape)


def read(slots, rows, cap):
    held = pl.BlockSpec(memory_space=pltpu.VMEM)
    return pl.pallas_call(
        functools.partial(read_kernel, cap),
        in_specs=[held] * 2,
        out_specs=held,
        out_shape=jax.ShapeDtypeStruct((8, 128), F32),
        compiler_params=pltpu.CompilerParams(vmem_limit_bytes=4 * 2**20),
        cost_estimate=pl.CostEstimate(flops=0, bytes_accessed=2**14, transcendentals=0),
        name="read",
    )(slots, rows)


def loss_kernel(mine_ref, other_ref, out_ref):
    lane = lax.broadcasted_iota(jnp.int32, (1, 128), 1)
    late = lax.axis_index("dp") % 2 == 1
    line = jnp.where(late, mine_ref[0:1, :], other_ref[0:1, :])
    out_ref[0, 0] = jnp.sum(jnp.where(lane < 3, line, 0.0))


def loss_of(mine, other):
    held = pl.BlockSpec(memory_space=pltpu.VMEM)
    far = pl.BlockSpec(memory_space=pltpu.SMEM)
    return pl.pallas_call(
        loss_kernel,
        in_specs=[held] * 2,
        out_specs=far,
        out_shape=jax.ShapeDtypeStruct((1, 1), F32),
        compiler_params=pltpu.CompilerParams(vmem_limit_bytes=2**20),
        name="loss",
    )(mine, other)


def combine_kernel(pick_ref, gates_ref, rows_ref, out_hbm, out_ref, sems):
    toks, width = out_ref.shape
    gates = gates_ref[...]
    labels = lax.broadcasted_iota(jnp.int32, (toks, toks), 0)
    lines = jnp.where(labels == 0, gates[0:1, :], jnp.where(labels == 1, gates[1:2, :], 0.0)).T
    first, second = lines[:, 0:1], lines[:, 1:2]
    block = width // PARTS
    copies = []
    for part in range(PARTS):
        tile = pl.ds(part * block, block)
        both = jnp.dot(pick_ref[...], rows_ref[:, tile], preferred_element_type=F32)
        out_ref[:, tile] = (first * both[:toks] + second * both[toks:]).astype(BF16)
        copies.append(
            pltpu.make_async_copy(out_ref.at[:, tile], out_hbm.at[:, tile], sems.at[part])
        )
        copies[-1].start()
    for copy in copies:
        copy.wait()


def combine(pick, gates, rows):
    toks = gates.shape[1]
    slots, width = rows.shape
    held = pl.BlockSpec(memory_space=pltpu.VMEM)
    return pl.pallas_call(
        combine_kernel,
        in_specs=[held] * 3,
        out_specs=pl.BlockSpec(memory_space=pltpu.HBM),
        out_shape=pltpu.HBM((toks, width), BF16),
        scratch_shapes=[pltpu.VMEM((toks, width), BF16), pltpu.SemaphoreType.DMA((PARTS,))],
        compiler_params=pltpu.CompilerParams(vmem_limit_bytes=16 * 2**20),
        cost_estimate=pl.CostEstimate(
            flops=4 * toks * slots * width, bytes_accessed=2 * slots * width, transcendentals=0
        ),
        name="combine",
    )(pick, gates, rows)


def add_round(value, size, step, partner):
    stride = 2 * step
    pairs = [
        (i, partner[i // stride] * stride + i % stride) for i in range(size) if (i // step) % 2 == 1
    ]
    return value + lax.ppermute(value, AXES, pairs)


def on_device(tokens, expert_ids, gate_weights, w_gate, w_up, w_down):
    toks, width = tokens.shape
    picks = expert_ids.shape[1]
    group = lax.axis_size("expert")
    copies = lax.axis_size("dp")
    experts = w_gate.shape[0] * group
    cap = min(toks * picks // 4, 3 * toks * picks // experts)
    all_tokens = toks * group * copies

    size = copies * group
    ids, gates = expert_ids.T, gate_weights.T
    slots, stats, tokens, gates = count(ids, gates, tokens, experts, cap)
    swap = [(i, i + group if (i // group) % 2 == 0 else i - group) for i in range(size)]
    late = lax.axis_index("dp") % 2
    other = lax.ppermute(stats, AXES, swap)
    outgoing = pack(slots, tokens, experts * cap)
    pick = select(slots, experts * cap)

    def column_sum(value, other):
        value = value + other
        for partner in ROUNDS:
            value = add_round(value, size, group, partner)
        return value

    stats = lax.cond(late == 1, column_sum, lambda value, other: value, stats, other)
    outgoing = note(slots, stats, outgoing, experts, cap)
    pick, outgoing = lax.optimization_barrier((pick, outgoing))
    received = lax.all_to_all(outgoing, "expert", split_axis=0, concat_axis=0, tiled=True)
    hidden, loss = hidden_of(slots, received, w_gate, w_up, experts, cap, all_tokens)
    result = down_of(slots, loss, hidden, w_down, cap)
    returned = lax.all_to_all(result, "expert", split_axis=0, concat_axis=0, tiled=True)
    loss = read(slots, returned, cap)
    other = lax.ppermute(loss, AXES, swap)
    mixed = combine(pick, gates, returned)
    other, mixed = lax.optimization_barrier((other, mixed))
    return mixed, loss_of(loss, other).reshape(())


def solution(mesh):
    rows = P(("dp", "expert"), None)
    held = P("expert", None, None)
    return jax.shard_map(
        on_device,
        mesh=mesh,
        in_specs=(rows, rows, rows, held, held, held),
        out_specs=(rows, P()),
        check_vma=False,
    )
```

```python
import functools

import jax
import jax.numpy as jnp
from jax import lax
from jax.experimental import pallas as pl
from jax.experimental.pallas import tpu as pltpu
from jax.sharding import PartitionSpec as P

F32 = jnp.float32
BF16 = jnp.bfloat16
PARTS = 4
ROUNDS = (
    (1, 0, 3, 2, 5, 4, 7, 6),
    (2, 3, 0, 1, 6, 7, 4, 5),
    (6, 7, 4, 5, 2, 3, 0, 1),
)
AXES = ("dp", "expert")


def slots_of(ids, experts, cap):
    toks = ids.shape[1]
    labels = lax.broadcasted_iota(jnp.int32, (experts, toks), 0)
    first = (labels == ids[0:1, :]).astype(F32)
    second = (labels == ids[1:2, :]).astype(F32)
    before = lax.broadcasted_iota(jnp.int32, (toks, toks), 0)
    earlier = (before < lax.broadcasted_iota(jnp.int32, (toks, toks), 1)).astype(F32).astype(BF16)
    both = jnp.concatenate([first, second], 0).astype(BF16)
    rank = jnp.dot(both, earlier, preferred_element_type=F32)
    first_rank, second_rank = rank[:experts], rank[experts:]
    first_count = jnp.sum(first, 1, keepdims=True)
    base = ids.astype(F32) * cap
    first_slot = base[0:1, :] + jnp.sum(first * first_rank, 0, keepdims=True)
    second_slot = base[1:2, :] + jnp.sum(second * (second_rank + first_count), 0, keepdims=True)
    return first_slot, second_slot, first, second


def count_kernel(
    experts, cap, ids_hbm, gates_hbm, tok_hbm, slot_ref, stats_ref, tok_ref, gates_ref, ids_ref, sems
):
    toks = ids_ref.shape[1]
    ids_copy = pltpu.make_async_copy(ids_hbm, ids_ref, sems.at[0])
    gates_copy = pltpu.make_async_copy(gates_hbm, gates_ref, sems.at[1])
    tok_copy = pltpu.make_async_copy(tok_hbm, tok_ref, sems.at[2])
    ids_copy.start()
    gates_copy.start()
    tok_copy.start()
    ids_copy.wait()
    first_slot, second_slot, first, second = slots_of(ids_ref[...], experts, cap)
    count = jnp.sum(first + second, 1, keepdims=True)
    gates_copy.wait()
    gates = gates_ref[...]
    mass = jnp.sum(first * gates[0:1, :] + second * gates[1:2, :], 1, keepdims=True)
    lanes = lax.broadcasted_iota(jnp.int32, (experts, toks), 1)
    stats = jnp.where(lanes == 0, count, jnp.where(lanes == 1, mass, 0.0))
    stats = jnp.concatenate([stats, jnp.zeros((toks - experts, toks), F32)], 0).T[:8, :]
    stats_ref[...] = stats
    lane = lax.broadcasted_iota(jnp.int32, (8, toks), 1)
    line = lax.broadcasted_iota(jnp.int32, (8, toks), 0)
    free = ((stats[0:1, :] < cap) & (lane < experts)).astype(jnp.int32)
    slots = jnp.where(line == 0, first_slot.astype(jnp.int32), second_slot.astype(jnp.int32))
    slot_ref[...] = jnp.where(line < 2, slots, free)
    tok_copy.wait()


def count(ids, gates, tokens, experts, cap):
    toks = ids.shape[1]
    return pl.pallas_call(
        functools.partial(count_kernel, experts, cap),
        in_specs=[pl.BlockSpec(memory_space=pltpu.HBM)] * 3,
        out_specs=[pl.BlockSpec(memory_space=pltpu.VMEM)] * 4,
        out_shape=[
            jax.ShapeDtypeStruct((8, toks), jnp.int32),
            jax.ShapeDtypeStruct((8, toks), F32),
            jax.ShapeDtypeStruct(tokens.shape, tokens.dtype),
            jax.ShapeDtypeStruct(gates.shape, gates.dtype),
        ],
        scratch_shapes=[
            pltpu.VMEM(ids.shape, ids.dtype),
            pltpu.SemaphoreType.DMA((3,)),
        ],
        compiler_params=pltpu.CompilerParams(vmem_limit_bytes=4 * 2**20),
        cost_estimate=pl.CostEstimate(flops=4 * toks**3, bytes_accessed=8 * toks, transcendentals=0),
        name="count",
    )(*(pltpu.with_memory_space_constraint(a, pltpu.HBM) for a in (ids, gates, tokens)))


def pieces(value, count):
    parts = []
    for _ in range(count):
        parts.append(value.astype(BF16).astype(F32))
        value = value - parts[-1]
    return parts


def pack_kernel(slot_ref, tok_ref, out_ref):
    toks = tok_ref.shape[0]
    rows = out_ref.shape[0] // PARTS
    tokens = tok_ref[...]
    first_slot, second_slot = slot_ref[0:1, :], slot_ref[1:2, :]
    for part in range(PARTS):
        slot = lax.broadcasted_iota(jnp.int32, (rows, toks), 0) + part * rows
        pick = ((slot == first_slot) | (slot == second_slot)).astype(F32).astype(BF16)
        out_ref[part * rows : (part + 1) * rows, :] = jnp.dot(
            pick, tokens, preferred_element_type=F32
        ).astype(BF16)


def pack(slots, tokens, count):
    toks, width = tokens.shape
    held = pl.BlockSpec(memory_space=pltpu.VMEM)
    return pl.pallas_call(
        pack_kernel,
        in_specs=[held] * 2,
        out_specs=held,
        out_shape=jax.ShapeDtypeStruct((count, width), BF16),
        compiler_params=pltpu.CompilerParams(vmem_limit_bytes=8 * 2**20),
        cost_estimate=pl.CostEstimate(
            flops=2 * count * toks * width, bytes_accessed=4 * count * width, transcendentals=0
        ),
        name="pack",
    )(slots, tokens)


def is_free(slot_ref, expert):
    lane = lax.broadcasted_iota(jnp.int32, (1, slot_ref.shape[1]), 1)
    return jnp.sum(jnp.where(lane == expert, slot_ref[2:3, :], 0), 1, keepdims=True) > 0


def note_kernel(experts, cap, slot_ref, sums_ref, in_ref, out_ref):
    lines = pieces(sums_ref[0:1, :], 2) + pieces(sums_ref[1:2, :], 3)
    line = jnp.concatenate(lines, 1)
    edge = line.shape[1]
    line = jnp.broadcast_to(line, (16, edge))
    last = lax.broadcasted_iota(jnp.int32, (16, edge), 0) == 15
    for e in range(experts):
        tile = slice((e + 1) * cap - 16, (e + 1) * cap)
        old = in_ref[tile, :edge].astype(F32)
        out_ref[tile, :edge] = jnp.where(last & is_free(slot_ref, e), line, old).astype(BF16)


def note(slots, sums, rows, experts, cap):
    held = pl.BlockSpec(memory_space=pltpu.VMEM)
    return pl.pallas_call(
        functools.partial(note_kernel, experts, cap),
        in_specs=[held] * 3,
        out_specs=held,
        out_shape=jax.ShapeDtypeStruct(rows.shape, rows.dtype),
        input_output_aliases={2: 0},
        compiler_params=pltpu.CompilerParams(vmem_limit_bytes=4 * 2**20),
        cost_estimate=pl.CostEstimate(flops=0, bytes_accessed=2**16, transcendentals=0),
        name="note",
    )(slots, sums, rows)


def hidden_kernel(experts, cap, tokens, slot_ref, x_ref, gate_ref, up_ref, out_ref, loss_ref, few_ref):
    lanes = loss_ref.shape[1]
    total = jnp.zeros((16, 5 * lanes), F32)
    for end in range(cap, x_ref.shape[0] + 1, cap):
        total = total + x_ref[end - 16 : end, : 5 * lanes].astype(F32)
    part = [total[15:16, i * lanes : (i + 1) * lanes] for i in range(5)]
    load, mass = part[0] + part[1], part[2] + part[3] + part[4]
    loss = experts * jnp.sum(load / (2 * tokens) * (mass / tokens), 1, keepdims=True)
    lane = lax.broadcasted_iota(jnp.int32, loss_ref.shape, 1)
    high, middle, low = pieces(loss, 3)
    line = jnp.where(lane == 0, high, jnp.where(lane == 1, middle, jnp.where(lane == 2, low, 0.0)))
    loss_ref[...] = line

    def run(rows_ref):
        rows = rows_ref.shape[0]
        x = rows_ref[...]
        for start in range(0, out_ref.shape[1], 256):
            tile = slice(start, start + 256)
            gate = jnp.dot(x, gate_ref[0, :, tile], preferred_element_type=F32)
            up = jnp.dot(x, up_ref[0, :, tile], preferred_element_type=F32)
            out_ref[:rows, tile] = (gate / (1.0 + jnp.exp(-gate)) * up).astype(BF16)

    free = mine_free(slot_ref)

    @pl.when(free)
    def _():
        for chunk in range(x_ref.shape[0] // cap):
            few_ref[chunk * 16 : chunk * 16 + 16, :] = x_ref[chunk * cap : chunk * cap + 16, :]
        run(few_ref)

    @pl.when(jnp.logical_not(free))
    def _():
        run(x_ref)


def mine_free(slot_ref):
    lane = lax.broadcasted_iota(jnp.int32, (1, slot_ref.shape[1]), 1)
    return jnp.sum(jnp.where(lane == lax.axis_index("expert"), slot_ref[2:3, :], 0)) > 0


def hidden_of(slots, x, w_gate, w_up, experts, cap, tokens):
    rows, width = x.shape
    middle = w_gate.shape[2]
    held = pl.BlockSpec(memory_space=pltpu.VMEM)
    return pl.pallas_call(
        functools.partial(hidden_kernel, experts, cap, tokens),
        in_specs=[held] * 4,
        out_specs=[held] * 2,
        out_shape=[jax.ShapeDtypeStruct((rows, middle), BF16), jax.ShapeDtypeStruct((8, 128), F32)],
        scratch_shapes=[pltpu.VMEM((rows // cap * 16, width), BF16)],
        compiler_params=pltpu.CompilerParams(vmem_limit_bytes=16 * 2**20),
        cost_estimate=pl.CostEstimate(
            flops=4 * rows * width * middle,
            bytes_accessed=2 * rows * width + 4 * width * middle,
            transcendentals=rows * middle,
        ),
        name="hidden",
    )(slots, x, w_gate, w_up)


def down_kernel(cap, slot_ref, loss_ref, x_ref, down_ref, out_ref):
    chunks = x_ref.shape[0] // cap
    free = mine_free(slot_ref)

    @pl.when(free)
    def _():
        few = chunks * 16
        rows = jnp.dot(x_ref[:few, :], down_ref[0], preferred_element_type=F32).astype(BF16)
        rest = jnp.zeros((cap - 16, out_ref.shape[1]), BF16)
        last = lax.broadcasted_iota(jnp.int32, (16, 128), 0) == 15
        line = jnp.broadcast_to(loss_ref[0:1, :], (16, 128))
        line = jnp.where(last, line, 0.0).astype(BF16)
        for chunk in range(chunks):
            start = chunk * cap
            out_ref[start : start + 16, :] = rows[chunk * 16 : chunk * 16 + 16, :]
            out_ref[start + 16 : start + cap, :] = rest
            out_ref[start + cap - 16 : start + cap, 0:128] = line

    @pl.when(jnp.logical_not(free))
    def _():
        for start in range(0, x_ref.shape[0], 256):
            tile = slice(start, start + 256)
            out_ref[tile, :] = jnp.dot(
                x_ref[tile, :], down_ref[0], preferred_element_type=F32
            ).astype(BF16)


def down_of(slots, loss, x, w_down, cap):
    rows, middle = x.shape
    width = w_down.shape[2]
    held = pl.BlockSpec(memory_space=pltpu.VMEM)
    return pl.pallas_call(
        functools.partial(down_kernel, cap),
        in_specs=[held] * 4,
        out_specs=held,
        out_shape=jax.ShapeDtypeStruct((rows, width), BF16),
        compiler_params=pltpu.CompilerParams(vmem_limit_bytes=16 * 2**20),
        cost_estimate=pl.CostEstimate(
            flops=2 * rows * width * middle,
            bytes_accessed=2 * rows * width + 2 * width * middle,
            transcendentals=0,
        ),
        name="down",
    )(slots, loss, x, w_down)


def select_kernel(slot_ref, pick_ref):
    toks, slots = slot_ref.shape[1], pick_ref.shape[1]
    labels = lax.broadcasted_iota(jnp.int32, (toks, toks), 0)
    first_slot, second_slot = slot_ref[0:1, :].astype(F32), slot_ref[1:2, :].astype(F32)
    lines = jnp.where(labels == 0, first_slot, jnp.where(labels == 1, second_slot, 0.0)).T
    dest = lines[:, 0:2].astype(jnp.int32)
    lane = lax.broadcasted_iota(jnp.int32, (toks, slots), 1)
    pick_ref[:toks, :] = (lane == dest[:, 0:1]).astype(F32).astype(BF16)
    pick_ref[toks:, :] = (lane == dest[:, 1:2]).astype(F32).astype(BF16)


def select(slots, count):
    toks = slots.shape[1]
    held = pl.BlockSpec(memory_space=pltpu.VMEM)
    return pl.pallas_call(
        select_kernel,
        in_specs=[held],
        out_specs=held,
        out_shape=jax.ShapeDtypeStruct((2 * toks, count), BF16),
        compiler_params=pltpu.CompilerParams(vmem_limit_bytes=4 * 2**20),
        cost_estimate=pl.CostEstimate(flops=0, bytes_accessed=4 * toks * count, transcendentals=0),
        name="select",
    )(slots)


def read_kernel(cap, slot_ref, rows_ref, out_ref):
    line = rows_ref[3 * cap - 16 : 3 * cap, 0:128].astype(F32)[15:16, :]
    for e in (1, 0):
        other = rows_ref[(e + 1) * cap - 16 : (e + 1) * cap, 0:128].astype(F32)[15:16, :]
        line = jnp.where(is_free(slot_ref, e), other, line)
    out_ref[...] = jnp.broadcast_to(line, out_ref.shape)


def read(slots, rows, cap):
    held = pl.BlockSpec(memory_space=pltpu.VMEM)
    return pl.pallas_call(
        functools.partial(read_kernel, cap),
        in_specs=[held] * 2,
        out_specs=held,
        out_shape=jax.ShapeDtypeStruct((8, 128), F32),
        compiler_params=pltpu.CompilerParams(vmem_limit_bytes=4 * 2**20),
        cost_estimate=pl.CostEstimate(flops=0, bytes_accessed=2**14, transcendentals=0),
        name="read",
    )(slots, rows)


def loss_kernel(mine_ref, other_ref, out_ref):
    lane = lax.broadcasted_iota(jnp.int32, (1, 128), 1)
    late = lax.axis_index("dp") % 2 == 1
    line = jnp.where(late, mine_ref[0:1, :], other_ref[0:1, :])
    out_ref[0, 0] = jnp.sum(jnp.where(lane < 3, line, 0.0))


def loss_of(mine, other):
    held = pl.BlockSpec(memory_space=pltpu.VMEM)
    far = pl.BlockSpec(memory_space=pltpu.SMEM)
    return pl.pallas_call(
        loss_kernel,
        in_specs=[held] * 2,
        out_specs=far,
        out_shape=jax.ShapeDtypeStruct((1, 1), F32),
        compiler_params=pltpu.CompilerParams(vmem_limit_bytes=2**20),
        name="loss",
    )(mine, other)


def combine_kernel(pick_ref, gates_ref, rows_ref, out_hbm, out_ref, sems):
    toks, width = out_ref.shape
    gates = gates_ref[...]
    labels = lax.broadcasted_iota(jnp.int32, (toks, toks), 0)
    lines = jnp.where(labels == 0, gates[0:1, :], jnp.where(labels == 1, gates[1:2, :], 0.0)).T
    first, second = lines[:, 0:1], lines[:, 1:2]
    block = width // PARTS
    copies = []
    for part in range(PARTS):
        tile = pl.ds(part * block, block)
        both = jnp.dot(pick_ref[...], rows_ref[:, tile], preferred_element_type=F32)
        out_ref[:, tile] = (first * both[:toks] + second * both[toks:]).astype(BF16)
        copies.append(
            pltpu.make_async_copy(out_ref.at[:, tile], out_hbm.at[:, tile], sems.at[part])
        )
        copies[-1].start()
    for copy in copies:
        copy.wait()


def combine(pick, gates, rows):
    toks = gates.shape[1]
    slots, width = rows.shape
    held = pl.BlockSpec(memory_space=pltpu.VMEM)
    return pl.pallas_call(
        combine_kernel,
        in_specs=[held] * 3,
        out_specs=pl.BlockSpec(memory_space=pltpu.HBM),
        out_shape=pltpu.HBM((toks, width), BF16),
        scratch_shapes=[pltpu.VMEM((toks, width), BF16), pltpu.SemaphoreType.DMA((PARTS,))],
        compiler_params=pltpu.CompilerParams(vmem_limit_bytes=16 * 2**20),
        cost_estimate=pl.CostEstimate(
            flops=4 * toks * slots * width, bytes_accessed=2 * slots * width, transcendentals=0
        ),
        name="combine",
    )(pick, gates, rows)


def add_round(value, size, step, partner):
    stride = 2 * step
    pairs = [
        (i, partner[i // stride] * stride + i % stride) for i in range(size) if (i // step) % 2 == 1
    ]
    return value + lax.ppermute(value, AXES, pairs)


def on_device(tokens, expert_ids, gate_weights, w_gate, w_up, w_down):
    toks, width = tokens.shape
    picks = expert_ids.shape[1]
    group = lax.axis_size("expert")
    copies = lax.axis_size("dp")
    experts = w_gate.shape[0] * group
    cap = min(toks * picks // 4, 3 * toks * picks // experts)
    all_tokens = toks * group * copies

    size = copies * group
    ids, gates = expert_ids.T, gate_weights.T
    slots, stats, tokens, gates = count(ids, gates, tokens, experts, cap)
    swap = [(i, i + group if (i // group) % 2 == 0 else i - group) for i in range(size)]
    late = lax.axis_index("dp") % 2
    other = lax.ppermute(stats, AXES, swap)
    outgoing = pack(slots, tokens, experts * cap)

    def column_sum(value, other, rows):
        value = value + other
        for partner in ROUNDS:
            value = add_round(value, size, group, partner)
        return note(slots, value, rows, experts, cap)

    outgoing = lax.cond(late == 1, column_sum, lambda value, other, rows: rows, stats, other, outgoing)
    received = lax.all_to_all(outgoing, "expert", split_axis=0, concat_axis=0, tiled=True)
    slots, received = lax.optimization_barrier((slots, received))
    pick = select(slots, experts * cap)
    received, pick = lax.optimization_barrier((received, pick))
    hidden, loss = hidden_of(slots, received, w_gate, w_up, experts, cap, all_tokens)
    result = down_of(slots, loss, hidden, w_down, cap)
    returned = lax.all_to_all(result, "expert", split_axis=0, concat_axis=0, tiled=True)
    loss = read(slots, returned, cap)
    other = lax.ppermute(loss, AXES, swap)
    mixed = combine(pick, gates, returned)
    other, mixed = lax.optimization_barrier((other, mixed))
    return mixed, loss_of(loss, other).reshape(())


def solution(mesh):
    rows = P(("dp", "expert"), None)
    held = P("expert", None, None)
    return jax.shard_map(
        on_device,
        mesh=mesh,
        in_specs=(rows, rows, rows, held, held, held),
        out_specs=(rows, P()),
        check_vma=False,
    )
```

```python
import functools

import jax
import jax.numpy as jnp
from jax import lax
from jax.experimental import pallas as pl
from jax.experimental.pallas import tpu as pltpu
from jax.sharding import PartitionSpec as P

F32 = jnp.float32
BF16 = jnp.bfloat16
PARTS = 4
ROUNDS = (
    (1, 0, 3, 2, 5, 4, 7, 6),
    (2, 3, 0, 1, 6, 7, 4, 5),
    (6, 7, 4, 5, 2, 3, 0, 1),
)
AXES = ("dp", "expert")


def slots_of(ids, experts, cap):
    toks = ids.shape[1]
    labels = lax.broadcasted_iota(jnp.int32, (experts, toks), 0)
    first = (labels == ids[0:1, :]).astype(F32)
    second = (labels == ids[1:2, :]).astype(F32)
    before = lax.broadcasted_iota(jnp.int32, (toks, toks), 0)
    earlier = (before < lax.broadcasted_iota(jnp.int32, (toks, toks), 1)).astype(F32).astype(BF16)
    both = jnp.concatenate([first, second], 0).astype(BF16)
    rank = jnp.dot(both, earlier, preferred_element_type=F32)
    first_rank, second_rank = rank[:experts], rank[experts:]
    first_count = jnp.sum(first, 1, keepdims=True)
    base = ids.astype(F32) * cap
    first_slot = base[0:1, :] + jnp.sum(first * first_rank, 0, keepdims=True)
    second_slot = base[1:2, :] + jnp.sum(second * (second_rank + first_count), 0, keepdims=True)
    return first_slot, second_slot, first, second


def count_kernel(
    experts, cap, ids_hbm, gates_hbm, tok_hbm, slot_ref, stats_ref, tok_ref, gates_ref, ids_ref, sems
):
    toks = ids_ref.shape[1]
    ids_copy = pltpu.make_async_copy(ids_hbm, ids_ref, sems.at[0])
    gates_copy = pltpu.make_async_copy(gates_hbm, gates_ref, sems.at[1])
    tok_copy = pltpu.make_async_copy(tok_hbm, tok_ref, sems.at[2])
    ids_copy.start()
    gates_copy.start()
    tok_copy.start()
    ids_copy.wait()
    first_slot, second_slot, first, second = slots_of(ids_ref[...], experts, cap)
    count = jnp.sum(first + second, 1, keepdims=True)
    gates_copy.wait()
    gates = gates_ref[...]
    mass = jnp.sum(first * gates[0:1, :] + second * gates[1:2, :], 1, keepdims=True)
    lanes = lax.broadcasted_iota(jnp.int32, (experts, toks), 1)
    stats = jnp.where(lanes == 0, count, jnp.where(lanes == 1, mass, 0.0))
    stats = jnp.concatenate([stats, jnp.zeros((toks - experts, toks), F32)], 0).T[:8, :]
    stats_ref[...] = stats
    lane = lax.broadcasted_iota(jnp.int32, (8, toks), 1)
    line = lax.broadcasted_iota(jnp.int32, (8, toks), 0)
    free = ((stats[0:1, :] < cap) & (lane < experts)).astype(jnp.int32)
    slots = jnp.where(line == 0, first_slot.astype(jnp.int32), second_slot.astype(jnp.int32))
    slot_ref[...] = jnp.where(line < 2, slots, free)
    tok_copy.wait()


def count(ids, gates, tokens, experts, cap):
    toks = ids.shape[1]
    return pl.pallas_call(
        functools.partial(count_kernel, experts, cap),
        in_specs=[pl.BlockSpec(memory_space=pltpu.HBM)] * 3,
        out_specs=[pl.BlockSpec(memory_space=pltpu.VMEM)] * 4,
        out_shape=[
            jax.ShapeDtypeStruct((8, toks), jnp.int32),
            jax.ShapeDtypeStruct((8, toks), F32),
            jax.ShapeDtypeStruct(tokens.shape, tokens.dtype),
            jax.ShapeDtypeStruct(gates.shape, gates.dtype),
        ],
        scratch_shapes=[
            pltpu.VMEM(ids.shape, ids.dtype),
            pltpu.SemaphoreType.DMA((3,)),
        ],
        compiler_params=pltpu.CompilerParams(vmem_limit_bytes=4 * 2**20),
        cost_estimate=pl.CostEstimate(flops=4 * toks**3, bytes_accessed=8 * toks, transcendentals=0),
        name="count",
    )(*(pltpu.with_memory_space_constraint(a, pltpu.HBM) for a in (ids, gates, tokens)))


def pieces(value, count):
    parts = []
    for _ in range(count):
        parts.append(value.astype(BF16).astype(F32))
        value = value - parts[-1]
    return parts


def pack_kernel(experts, cap, slot_ref, tok_ref, out_ref):
    toks = tok_ref.shape[0]
    few, rest = experts * 16, cap - 16
    first_slot, second_slot = slot_ref[0:1, :], slot_ref[1:2, :]
    lane = lax.broadcasted_iota(jnp.int32, (1, toks), 1)
    full = (lane < experts) & (slot_ref[2:3, :] == 0)
    low = jnp.min(jnp.where(full, lane, experts - 1))
    high = jnp.max(jnp.where(full, lane, 0))
    row = lax.broadcasted_iota(jnp.int32, (few, toks), 0)
    slot = (row >> 4) * cap + (row & 15)
    pick = ((slot == first_slot) | (slot == second_slot)).astype(F32).astype(BF16)
    rows = jnp.dot(pick, tok_ref[...], preferred_element_type=F32).astype(BF16)
    none = jnp.zeros((rest, out_ref.shape[1]), BF16)
    for e in range(experts):
        out_ref[e * cap : e * cap + 16, :] = rows[e * 16 : e * 16 + 16, :]
        out_ref[e * cap + 16 : (e + 1) * cap, :] = none
    for expert in (low, high):
        start = pl.multiple_of(expert * cap + 16, 16)
        slot = lax.broadcasted_iota(jnp.int32, (rest, toks), 0) + start
        pick = ((slot == first_slot) | (slot == second_slot)).astype(F32).astype(BF16)
        out_ref[pl.ds(start, rest), :] = jnp.dot(
            pick, tok_ref[...], preferred_element_type=F32
        ).astype(BF16)


def pack(slots, tokens, experts, cap):
    toks, width = tokens.shape
    count = experts * cap
    held = pl.BlockSpec(memory_space=pltpu.VMEM)
    return pl.pallas_call(
        functools.partial(pack_kernel, experts, cap),
        in_specs=[held] * 2,
        out_specs=held,
        out_shape=jax.ShapeDtypeStruct((count, width), BF16),
        compiler_params=pltpu.CompilerParams(vmem_limit_bytes=8 * 2**20),
        cost_estimate=pl.CostEstimate(
            flops=2 * count * toks * width, bytes_accessed=4 * count * width, transcendentals=0
        ),
        name="pack",
    )(slots, tokens)


def is_free(slot_ref, expert):
    lane = lax.broadcasted_iota(jnp.int32, (1, slot_ref.shape[1]), 1)
    return jnp.sum(jnp.where(lane == expert, slot_ref[2:3, :], 0), 1, keepdims=True) > 0


def note_kernel(experts, cap, slot_ref, sums_ref, in_ref, out_ref):
    lines = pieces(sums_ref[0:1, :], 2) + pieces(sums_ref[1:2, :], 3)
    line = jnp.concatenate(lines, 1)
    edge = line.shape[1]
    line = jnp.broadcast_to(line, (16, edge))
    last = lax.broadcasted_iota(jnp.int32, (16, edge), 0) == 15
    for e in range(experts):
        tile = slice((e + 1) * cap - 16, (e + 1) * cap)
        old = in_ref[tile, :edge].astype(F32)
        out_ref[tile, :edge] = jnp.where(last & is_free(slot_ref, e), line, old).astype(BF16)


def note(slots, sums, rows, experts, cap):
    held = pl.BlockSpec(memory_space=pltpu.VMEM)
    return pl.pallas_call(
        functools.partial(note_kernel, experts, cap),
        in_specs=[held] * 3,
        out_specs=held,
        out_shape=jax.ShapeDtypeStruct(rows.shape, rows.dtype),
        input_output_aliases={2: 0},
        compiler_params=pltpu.CompilerParams(vmem_limit_bytes=4 * 2**20),
        cost_estimate=pl.CostEstimate(flops=0, bytes_accessed=2**16, transcendentals=0),
        name="note",
    )(slots, sums, rows)


def hidden_kernel(experts, cap, tokens, slot_ref, x_ref, gate_ref, up_ref, out_ref, loss_ref, few_ref):
    lanes = loss_ref.shape[1]
    total = jnp.zeros((16, 5 * lanes), F32)
    for end in range(cap, x_ref.shape[0] + 1, cap):
        total = total + x_ref[end - 16 : end, : 5 * lanes].astype(F32)
    part = [total[15:16, i * lanes : (i + 1) * lanes] for i in range(5)]
    load, mass = part[0] + part[1], part[2] + part[3] + part[4]
    loss = experts * jnp.sum(load / (2 * tokens) * (mass / tokens), 1, keepdims=True)
    lane = lax.broadcasted_iota(jnp.int32, loss_ref.shape, 1)
    high, middle, low = pieces(loss, 3)
    line = jnp.where(lane == 0, high, jnp.where(lane == 1, middle, jnp.where(lane == 2, low, 0.0)))
    loss_ref[...] = line

    def run(rows_ref):
        rows = rows_ref.shape[0]
        x = rows_ref[...]
        for start in range(0, out_ref.shape[1], 256):
            tile = slice(start, start + 256)
            gate = jnp.dot(x, gate_ref[0, :, tile], preferred_element_type=F32)
            up = jnp.dot(x, up_ref[0, :, tile], preferred_element_type=F32)
            out_ref[:rows, tile] = (gate / (1.0 + jnp.exp(-gate)) * up).astype(BF16)

    free = mine_free(slot_ref)

    @pl.when(free)
    def _():
        for chunk in range(x_ref.shape[0] // cap):
            few_ref[chunk * 16 : chunk * 16 + 16, :] = x_ref[chunk * cap : chunk * cap + 16, :]
        run(few_ref)

    @pl.when(jnp.logical_not(free))
    def _():
        run(x_ref)


def mine_free(slot_ref):
    lane = lax.broadcasted_iota(jnp.int32, (1, slot_ref.shape[1]), 1)
    return jnp.sum(jnp.where(lane == lax.axis_index("expert"), slot_ref[2:3, :], 0)) > 0


def hidden_of(slots, x, w_gate, w_up, experts, cap, tokens):
    rows, width = x.shape
    middle = w_gate.shape[2]
    held = pl.BlockSpec(memory_space=pltpu.VMEM)
    return pl.pallas_call(
        functools.partial(hidden_kernel, experts, cap, tokens),
        in_specs=[held] * 4,
        out_specs=[held] * 2,
        out_shape=[jax.ShapeDtypeStruct((rows, middle), BF16), jax.ShapeDtypeStruct((8, 128), F32)],
        scratch_shapes=[pltpu.VMEM((rows // cap * 16, width), BF16)],
        compiler_params=pltpu.CompilerParams(vmem_limit_bytes=16 * 2**20),
        cost_estimate=pl.CostEstimate(
            flops=4 * rows * width * middle,
            bytes_accessed=2 * rows * width + 4 * width * middle,
            transcendentals=rows * middle,
        ),
        name="hidden",
    )(slots, x, w_gate, w_up)


def down_kernel(cap, slot_ref, loss_ref, x_ref, down_ref, out_ref):
    chunks = x_ref.shape[0] // cap
    free = mine_free(slot_ref)

    @pl.when(free)
    def _():
        few = chunks * 16
        rows = jnp.dot(x_ref[:few, :], down_ref[0], preferred_element_type=F32).astype(BF16)
        rest = jnp.zeros((cap - 16, out_ref.shape[1]), BF16)
        last = lax.broadcasted_iota(jnp.int32, (16, 128), 0) == 15
        line = jnp.broadcast_to(loss_ref[0:1, :], (16, 128))
        line = jnp.where(last, line, 0.0).astype(BF16)
        for chunk in range(chunks):
            start = chunk * cap
            out_ref[start : start + 16, :] = rows[chunk * 16 : chunk * 16 + 16, :]
            out_ref[start + 16 : start + cap, :] = rest
            out_ref[start + cap - 16 : start + cap, 0:128] = line

    @pl.when(jnp.logical_not(free))
    def _():
        for start in range(0, x_ref.shape[0], 256):
            tile = slice(start, start + 256)
            out_ref[tile, :] = jnp.dot(
                x_ref[tile, :], down_ref[0], preferred_element_type=F32
            ).astype(BF16)


def down_of(slots, loss, x, w_down, cap):
    rows, middle = x.shape
    width = w_down.shape[2]
    held = pl.BlockSpec(memory_space=pltpu.VMEM)
    return pl.pallas_call(
        functools.partial(down_kernel, cap),
        in_specs=[held] * 4,
        out_specs=held,
        out_shape=jax.ShapeDtypeStruct((rows, width), BF16),
        compiler_params=pltpu.CompilerParams(vmem_limit_bytes=16 * 2**20),
        cost_estimate=pl.CostEstimate(
            flops=2 * rows * width * middle,
            bytes_accessed=2 * rows * width + 2 * width * middle,
            transcendentals=0,
        ),
        name="down",
    )(slots, loss, x, w_down)


def select_kernel(slot_ref, pick_ref):
    toks, slots = slot_ref.shape[1], pick_ref.shape[1]
    labels = lax.broadcasted_iota(jnp.int32, (toks, toks), 0)
    first_slot, second_slot = slot_ref[0:1, :].astype(F32), slot_ref[1:2, :].astype(F32)
    lines = jnp.where(labels == 0, first_slot, jnp.where(labels == 1, second_slot, 0.0)).T
    dest = lines[:, 0:2].astype(jnp.int32)
    lane = lax.broadcasted_iota(jnp.int32, (toks, slots), 1)
    pick_ref[:toks, :] = (lane == dest[:, 0:1]).astype(F32).astype(BF16)
    pick_ref[toks:, :] = (lane == dest[:, 1:2]).astype(F32).astype(BF16)


def select(slots, count):
    toks = slots.shape[1]
    held = pl.BlockSpec(memory_space=pltpu.VMEM)
    return pl.pallas_call(
        select_kernel,
        in_specs=[held],
        out_specs=held,
        out_shape=jax.ShapeDtypeStruct((2 * toks, count), BF16),
        compiler_params=pltpu.CompilerParams(vmem_limit_bytes=4 * 2**20),
        cost_estimate=pl.CostEstimate(flops=0, bytes_accessed=4 * toks * count, transcendentals=0),
        name="select",
    )(slots)


def read_kernel(cap, slot_ref, rows_ref, out_ref):
    line = rows_ref[3 * cap - 16 : 3 * cap, 0:128].astype(F32)[15:16, :]
    for e in (1, 0):
        other = rows_ref[(e + 1) * cap - 16 : (e + 1) * cap, 0:128].astype(F32)[15:16, :]
        line = jnp.where(is_free(slot_ref, e), other, line)
    out_ref[...] = jnp.broadcast_to(line, out_ref.shape)


def read(slots, rows, cap):
    held = pl.BlockSpec(memory_space=pltpu.VMEM)
    return pl.pallas_call(
        functools.partial(read_kernel, cap),
        in_specs=[held] * 2,
        out_specs=held,
        out_shape=jax.ShapeDtypeStruct((8, 128), F32),
        compiler_params=pltpu.CompilerParams(vmem_limit_bytes=4 * 2**20),
        cost_estimate=pl.CostEstimate(flops=0, bytes_accessed=2**14, transcendentals=0),
        name="read",
    )(slots, rows)


def loss_kernel(mine_ref, other_ref, out_ref):
    lane = lax.broadcasted_iota(jnp.int32, (1, 128), 1)
    late = lax.axis_index("dp") % 2 == 1
    line = jnp.where(late, mine_ref[0:1, :], other_ref[0:1, :])
    out_ref[0, 0] = jnp.sum(jnp.where(lane < 3, line, 0.0))


def loss_of(mine, other):
    held = pl.BlockSpec(memory_space=pltpu.VMEM)
    far = pl.BlockSpec(memory_space=pltpu.SMEM)
    return pl.pallas_call(
        loss_kernel,
        in_specs=[held] * 2,
        out_specs=far,
        out_shape=jax.ShapeDtypeStruct((1, 1), F32),
        compiler_params=pltpu.CompilerParams(vmem_limit_bytes=2**20),
        name="loss",
    )(mine, other)


def combine_kernel(pick_ref, gates_ref, rows_ref, out_hbm, out_ref, sems):
    toks, width = out_ref.shape
    gates = gates_ref[...]
    labels = lax.broadcasted_iota(jnp.int32, (toks, toks), 0)
    lines = jnp.where(labels == 0, gates[0:1, :], jnp.where(labels == 1, gates[1:2, :], 0.0)).T
    first, second = lines[:, 0:1], lines[:, 1:2]
    block = width // PARTS
    copies = []
    for part in range(PARTS):
        tile = pl.ds(part * block, block)
        both = jnp.dot(pick_ref[...], rows_ref[:, tile], preferred_element_type=F32)
        out_ref[:, tile] = (first * both[:toks] + second * both[toks:]).astype(BF16)
        copies.append(
            pltpu.make_async_copy(out_ref.at[:, tile], out_hbm.at[:, tile], sems.at[part])
        )
        copies[-1].start()
    for copy in copies:
        copy.wait()


def combine(pick, gates, rows):
    toks = gates.shape[1]
    slots, width = rows.shape
    held = pl.BlockSpec(memory_space=pltpu.VMEM)
    return pl.pallas_call(
        combine_kernel,
        in_specs=[held] * 3,
        out_specs=pl.BlockSpec(memory_space=pltpu.HBM),
        out_shape=pltpu.HBM((toks, width), BF16),
        scratch_shapes=[pltpu.VMEM((toks, width), BF16), pltpu.SemaphoreType.DMA((PARTS,))],
        compiler_params=pltpu.CompilerParams(vmem_limit_bytes=16 * 2**20),
        cost_estimate=pl.CostEstimate(
            flops=4 * toks * slots * width, bytes_accessed=2 * slots * width, transcendentals=0
        ),
        name="combine",
    )(pick, gates, rows)


def add_round(value, size, step, partner):
    stride = 2 * step
    pairs = [
        (i, partner[i // stride] * stride + i % stride) for i in range(size) if (i // step) % 2 == 1
    ]
    return value + lax.ppermute(value, AXES, pairs)


def on_device(tokens, expert_ids, gate_weights, w_gate, w_up, w_down):
    toks, width = tokens.shape
    picks = expert_ids.shape[1]
    group = lax.axis_size("expert")
    copies = lax.axis_size("dp")
    experts = w_gate.shape[0] * group
    cap = min(toks * picks // 4, 3 * toks * picks // experts)
    all_tokens = toks * group * copies

    size = copies * group
    ids, gates = expert_ids.T, gate_weights.T
    slots, stats, tokens, gates = count(ids, gates, tokens, experts, cap)
    swap = [(i, i + group if (i // group) % 2 == 0 else i - group) for i in range(size)]
    late = lax.axis_index("dp") % 2
    other = lax.ppermute(stats, AXES, swap)
    outgoing = pack(slots, tokens, experts, cap)

    def column_sum(value, other, rows):
        value = value + other
        for partner in ROUNDS:
            value = add_round(value, size, group, partner)
        return note(slots, value, rows, experts, cap)

    outgoing = lax.cond(late == 1, column_sum, lambda value, other, rows: rows, stats, other, outgoing)
    received = lax.all_to_all(outgoing, "expert", split_axis=0, concat_axis=0, tiled=True)
    slots, received = lax.optimization_barrier((slots, received))
    pick = select(slots, experts * cap)
    received, pick = lax.optimization_barrier((received, pick))
    hidden, loss = hidden_of(slots, received, w_gate, w_up, experts, cap, all_tokens)
    result = down_of(slots, loss, hidden, w_down, cap)
    returned = lax.all_to_all(result, "expert", split_axis=0, concat_axis=0, tiled=True)
    loss = read(slots, returned, cap)
    other = lax.ppermute(loss, AXES, swap)
    mixed = combine(pick, gates, returned)
    other, mixed = lax.optimization_barrier((other, mixed))
    return mixed, loss_of(loss, other).reshape(())


def solution(mesh):
    rows = P(("dp", "expert"), None)
    held = P("expert", None, None)
    return jax.shard_map(
        on_device,
        mesh=mesh,
        in_specs=(rows, rows, rows, held, held, held),
        out_specs=(rows, P()),
        check_vma=False,
    )
```

```python
import functools

import jax
import jax.numpy as jnp
from jax import lax
from jax.experimental import pallas as pl
from jax.experimental.pallas import tpu as pltpu
from jax.sharding import PartitionSpec as P

F32 = jnp.float32
BF16 = jnp.bfloat16
PARTS = 4
ROUNDS = (
    (1, 0, 3, 2, 5, 4, 7, 6),
    (2, 3, 0, 1, 6, 7, 4, 5),
    (6, 7, 4, 5, 2, 3, 0, 1),
)
AXES = ("dp", "expert")


def slots_of(ids, experts, cap):
    toks = ids.shape[1]
    labels = lax.broadcasted_iota(jnp.int32, (experts, toks), 0)
    first = (labels == ids[0:1, :]).astype(F32)
    second = (labels == ids[1:2, :]).astype(F32)
    before = lax.broadcasted_iota(jnp.int32, (toks, toks), 0)
    earlier = (before < lax.broadcasted_iota(jnp.int32, (toks, toks), 1)).astype(F32).astype(BF16)
    both = jnp.concatenate([first, second], 0).astype(BF16)
    rank = jnp.dot(both, earlier, preferred_element_type=F32)
    first_rank, second_rank = rank[:experts], rank[experts:]
    first_count = jnp.sum(first, 1, keepdims=True)
    base = ids.astype(F32) * cap
    first_slot = base[0:1, :] + jnp.sum(first * first_rank, 0, keepdims=True)
    second_slot = base[1:2, :] + jnp.sum(second * (second_rank + first_count), 0, keepdims=True)
    return first_slot, second_slot, first, second


def count_kernel(
    experts, cap, ids_hbm, gates_hbm, tok_hbm, slot_ref, stats_ref, tok_ref, gates_ref, ids_ref, sems
):
    toks = ids_ref.shape[1]
    ids_copy = pltpu.make_async_copy(ids_hbm, ids_ref, sems.at[0])
    gates_copy = pltpu.make_async_copy(gates_hbm, gates_ref, sems.at[1])
    tok_copy = pltpu.make_async_copy(tok_hbm, tok_ref, sems.at[2])
    ids_copy.start()
    gates_copy.start()
    tok_copy.start()
    ids_copy.wait()
    first_slot, second_slot, first, second = slots_of(ids_ref[...], experts, cap)
    count = jnp.sum(first + second, 1, keepdims=True)
    gates_copy.wait()
    gates = gates_ref[...]
    mass = jnp.sum(first * gates[0:1, :] + second * gates[1:2, :], 1, keepdims=True)
    lanes = lax.broadcasted_iota(jnp.int32, (experts, toks), 1)
    stats = jnp.where(lanes == 0, count, jnp.where(lanes == 1, mass, 0.0))
    stats = jnp.concatenate([stats, jnp.zeros((toks - experts, toks), F32)], 0).T[:8, :]
    stats_ref[...] = stats
    lane = lax.broadcasted_iota(jnp.int32, (8, toks), 1)
    line = lax.broadcasted_iota(jnp.int32, (8, toks), 0)
    free = ((stats[0:1, :] < cap) & (lane < experts)).astype(jnp.int32)
    slots = jnp.where(line == 0, first_slot.astype(jnp.int32), second_slot.astype(jnp.int32))
    slot_ref[...] = jnp.where(line < 2, slots, free)
    tok_copy.wait()


def count(ids, gates, tokens, experts, cap):
    toks = ids.shape[1]
    return pl.pallas_call(
        functools.partial(count_kernel, experts, cap),
        in_specs=[pl.BlockSpec(memory_space=pltpu.HBM)] * 3,
        out_specs=[pl.BlockSpec(memory_space=pltpu.VMEM)] * 4,
        out_shape=[
            jax.ShapeDtypeStruct((8, toks), jnp.int32),
            jax.ShapeDtypeStruct((8, toks), F32),
            jax.ShapeDtypeStruct(tokens.shape, tokens.dtype),
            jax.ShapeDtypeStruct(gates.shape, gates.dtype),
        ],
        scratch_shapes=[
            pltpu.VMEM(ids.shape, ids.dtype),
            pltpu.SemaphoreType.DMA((3,)),
        ],
        compiler_params=pltpu.CompilerParams(vmem_limit_bytes=4 * 2**20),
        cost_estimate=pl.CostEstimate(flops=4 * toks**3, bytes_accessed=8 * toks, transcendentals=0),
        name="count",
    )(*(pltpu.with_memory_space_constraint(a, pltpu.HBM) for a in (ids, gates, tokens)))


def pieces(value, count):
    parts = []
    for _ in range(count):
        parts.append(value.astype(BF16).astype(F32))
        value = value - parts[-1]
    return parts


def pack_kernel(slot_ref, tok_ref, out_ref):
    toks = tok_ref.shape[0]
    rows = out_ref.shape[0] // PARTS
    tokens = tok_ref[...]
    first_slot, second_slot = slot_ref[0:1, :], slot_ref[1:2, :]
    for part in range(PARTS):
        slot = lax.broadcasted_iota(jnp.int32, (rows, toks), 0) + part * rows
        pick = ((slot == first_slot) | (slot == second_slot)).astype(F32).astype(BF16)
        out_ref[part * rows : (part + 1) * rows, :] = jnp.dot(
            pick, tokens, preferred_element_type=F32
        ).astype(BF16)


def pack(slots, tokens, count):
    toks, width = tokens.shape
    held = pl.BlockSpec(memory_space=pltpu.VMEM)
    return pl.pallas_call(
        pack_kernel,
        in_specs=[held] * 2,
        out_specs=held,
        out_shape=jax.ShapeDtypeStruct((count, width), BF16),
        compiler_params=pltpu.CompilerParams(vmem_limit_bytes=8 * 2**20),
        cost_estimate=pl.CostEstimate(
            flops=2 * count * toks * width, bytes_accessed=4 * count * width, transcendentals=0
        ),
        name="pack",
    )(slots, tokens)


def is_free(slot_ref, expert):
    lane = lax.broadcasted_iota(jnp.int32, (1, slot_ref.shape[1]), 1)
    return jnp.sum(jnp.where(lane == expert, slot_ref[2:3, :], 0), 1, keepdims=True) > 0


def note_kernel(experts, cap, slot_ref, sums_ref, in_ref, out_ref):
    lines = pieces(sums_ref[0:1, :], 2) + pieces(sums_ref[1:2, :], 3)
    line = jnp.concatenate(lines, 1)
    edge = line.shape[1]
    line = jnp.broadcast_to(line, (16, edge))
    last = lax.broadcasted_iota(jnp.int32, (16, edge), 0) == 15
    for e in range(experts):
        tile = slice((e + 1) * cap - 16, (e + 1) * cap)
        old = in_ref[tile, :edge].astype(F32)
        out_ref[tile, :edge] = jnp.where(last & is_free(slot_ref, e), line, old).astype(BF16)


def note(slots, sums, rows, experts, cap):
    held = pl.BlockSpec(memory_space=pltpu.VMEM)
    return pl.pallas_call(
        functools.partial(note_kernel, experts, cap),
        in_specs=[held] * 3,
        out_specs=held,
        out_shape=jax.ShapeDtypeStruct(rows.shape, rows.dtype),
        input_output_aliases={2: 0},
        compiler_params=pltpu.CompilerParams(vmem_limit_bytes=4 * 2**20),
        cost_estimate=pl.CostEstimate(flops=0, bytes_accessed=2**16, transcendentals=0),
        name="note",
    )(slots, sums, rows)


def hidden_kernel(experts, cap, tokens, slot_ref, x_ref, gate_ref, up_ref, out_ref, loss_ref, few_ref):
    lanes = loss_ref.shape[1]
    total = jnp.zeros((16, 5 * lanes), F32)
    for end in range(cap, x_ref.shape[0] + 1, cap):
        total = total + x_ref[end - 16 : end, : 5 * lanes].astype(F32)
    part = [total[15:16, i * lanes : (i + 1) * lanes] for i in range(5)]
    load, mass = part[0] + part[1], part[2] + part[3] + part[4]
    loss = experts * jnp.sum(load / (2 * tokens) * (mass / tokens), 1, keepdims=True)
    lane = lax.broadcasted_iota(jnp.int32, loss_ref.shape, 1)
    high, middle, low = pieces(loss, 3)
    line = jnp.where(lane == 0, high, jnp.where(lane == 1, middle, jnp.where(lane == 2, low, 0.0)))
    loss_ref[...] = line

    def run(rows_ref):
        rows = rows_ref.shape[0]
        x = rows_ref[...]
        for start in range(0, out_ref.shape[1], 256):
            tile = slice(start, start + 256)
            gate = jnp.dot(x, gate_ref[0, :, tile], preferred_element_type=F32)
            up = jnp.dot(x, up_ref[0, :, tile], preferred_element_type=F32)
            out_ref[:rows, tile] = (gate / (1.0 + jnp.exp(-gate)) * up).astype(BF16)

    free = mine_free(slot_ref)

    @pl.when(free)
    def _():
        for chunk in range(x_ref.shape[0] // cap):
            few_ref[chunk * 16 : chunk * 16 + 16, :] = x_ref[chunk * cap : chunk * cap + 16, :]
        run(few_ref)

    @pl.when(jnp.logical_not(free))
    def _():
        run(x_ref)


def mine_free(slot_ref):
    lane = lax.broadcasted_iota(jnp.int32, (1, slot_ref.shape[1]), 1)
    return jnp.sum(jnp.where(lane == lax.axis_index("expert"), slot_ref[2:3, :], 0)) > 0


def hidden_of(slots, x, w_gate, w_up, experts, cap, tokens):
    rows, width = x.shape
    middle = w_gate.shape[2]
    held = pl.BlockSpec(memory_space=pltpu.VMEM)
    return pl.pallas_call(
        functools.partial(hidden_kernel, experts, cap, tokens),
        in_specs=[held] * 4,
        out_specs=[held] * 2,
        out_shape=[jax.ShapeDtypeStruct((rows, middle), BF16), jax.ShapeDtypeStruct((8, 128), F32)],
        scratch_shapes=[pltpu.VMEM((rows // cap * 16, width), BF16)],
        compiler_params=pltpu.CompilerParams(vmem_limit_bytes=16 * 2**20),
        cost_estimate=pl.CostEstimate(
            flops=4 * rows * width * middle,
            bytes_accessed=2 * rows * width + 4 * width * middle,
            transcendentals=rows * middle,
        ),
        name="hidden",
    )(slots, x, w_gate, w_up)


def down_kernel(cap, slot_ref, loss_ref, x_ref, down_ref, out_ref):
    chunks = x_ref.shape[0] // cap
    free = mine_free(slot_ref)

    @pl.when(free)
    def _():
        few = chunks * 16
        rows = jnp.dot(x_ref[:few, :], down_ref[0], preferred_element_type=F32).astype(BF16)
        rest = jnp.zeros((cap - 16, out_ref.shape[1]), BF16)
        last = lax.broadcasted_iota(jnp.int32, (16, 128), 0) == 15
        line = jnp.broadcast_to(loss_ref[0:1, :], (16, 128))
        line = jnp.where(last, line, 0.0).astype(BF16)
        for chunk in range(chunks):
            start = chunk * cap
            out_ref[start : start + 16, :] = rows[chunk * 16 : chunk * 16 + 16, :]
            out_ref[start + 16 : start + cap, :] = rest
            out_ref[start + cap - 16 : start + cap, 0:128] = line

    @pl.when(jnp.logical_not(free))
    def _():
        for start in range(0, x_ref.shape[0], 256):
            tile = slice(start, start + 256)
            out_ref[tile, :] = jnp.dot(
                x_ref[tile, :], down_ref[0], preferred_element_type=F32
            ).astype(BF16)


def down_of(slots, loss, x, w_down, cap):
    rows, middle = x.shape
    width = w_down.shape[2]
    held = pl.BlockSpec(memory_space=pltpu.VMEM)
    return pl.pallas_call(
        functools.partial(down_kernel, cap),
        in_specs=[held] * 4,
        out_specs=held,
        out_shape=jax.ShapeDtypeStruct((rows, width), BF16),
        compiler_params=pltpu.CompilerParams(vmem_limit_bytes=16 * 2**20),
        cost_estimate=pl.CostEstimate(
            flops=2 * rows * width * middle,
            bytes_accessed=2 * rows * width + 2 * width * middle,
            transcendentals=0,
        ),
        name="down",
    )(slots, loss, x, w_down)


def select_kernel(slot_ref, gates_ref, pick_ref, weight_ref):
    toks, slots = slot_ref.shape[1], pick_ref.shape[1]
    labels = lax.broadcasted_iota(jnp.int32, (toks, toks), 0)
    first_slot, second_slot = slot_ref[0:1, :].astype(F32), slot_ref[1:2, :].astype(F32)
    gates = gates_ref[...]
    lines = jnp.where(labels == 0, first_slot, jnp.where(labels == 1, second_slot, 0.0))
    lines = jnp.where(labels == 2, gates[0:1, :], jnp.where(labels == 3, gates[1:2, :], lines)).T
    weight_ref[...] = lines
    dest = lines[:, 0:2].astype(jnp.int32)
    lane = lax.broadcasted_iota(jnp.int32, (toks, slots), 1)
    pick_ref[:toks, :] = (lane == dest[:, 0:1]).astype(F32).astype(BF16)
    pick_ref[toks:, :] = (lane == dest[:, 1:2]).astype(F32).astype(BF16)


def select(slots, gates, count):
    toks = slots.shape[1]
    held = pl.BlockSpec(memory_space=pltpu.VMEM)
    return pl.pallas_call(
        select_kernel,
        in_specs=[held] * 2,
        out_specs=[held] * 2,
        out_shape=[
            jax.ShapeDtypeStruct((2 * toks, count), BF16),
            jax.ShapeDtypeStruct((toks, toks), F32),
        ],
        compiler_params=pltpu.CompilerParams(vmem_limit_bytes=4 * 2**20),
        cost_estimate=pl.CostEstimate(flops=0, bytes_accessed=4 * toks * count, transcendentals=0),
        name="select",
    )(slots, gates)


def read_kernel(cap, slot_ref, rows_ref, out_ref):
    line = rows_ref[3 * cap - 16 : 3 * cap, 0:128].astype(F32)[15:16, :]
    for e in (1, 0):
        other = rows_ref[(e + 1) * cap - 16 : (e + 1) * cap, 0:128].astype(F32)[15:16, :]
        line = jnp.where(is_free(slot_ref, e), other, line)
    out_ref[...] = jnp.broadcast_to(line, out_ref.shape)


def read(slots, rows, cap):
    held = pl.BlockSpec(memory_space=pltpu.VMEM)
    return pl.pallas_call(
        functools.partial(read_kernel, cap),
        in_specs=[held] * 2,
        out_specs=held,
        out_shape=jax.ShapeDtypeStruct((8, 128), F32),
        compiler_params=pltpu.CompilerParams(vmem_limit_bytes=4 * 2**20),
        cost_estimate=pl.CostEstimate(flops=0, bytes_accessed=2**14, transcendentals=0),
        name="read",
    )(slots, rows)


def loss_kernel(mine_ref, other_ref, out_ref):
    lane = lax.broadcasted_iota(jnp.int32, (1, 128), 1)
    late = lax.axis_index("dp") % 2 == 1
    line = jnp.where(late, mine_ref[0:1, :], other_ref[0:1, :])
    out_ref[0, 0] = jnp.sum(jnp.where(lane < 3, line, 0.0))


def loss_of(mine, other):
    held = pl.BlockSpec(memory_space=pltpu.VMEM)
    far = pl.BlockSpec(memory_space=pltpu.SMEM)
    return pl.pallas_call(
        loss_kernel,
        in_specs=[held] * 2,
        out_specs=far,
        out_shape=jax.ShapeDtypeStruct((1, 1), F32),
        compiler_params=pltpu.CompilerParams(vmem_limit_bytes=2**20),
        name="loss",
    )(mine, other)


def combine_kernel(pick_ref, weight_ref, rows_ref, out_hbm, out_ref, sems):
    toks, width = out_ref.shape
    first, second = weight_ref[:, 2:3], weight_ref[:, 3:4]
    block = width // PARTS
    copies = []
    for part in range(PARTS):
        tile = pl.ds(part * block, block)
        both = jnp.dot(pick_ref[...], rows_ref[:, tile], preferred_element_type=F32)
        out_ref[:, tile] = (first * both[:toks] + second * both[toks:]).astype(BF16)
        copies.append(
            pltpu.make_async_copy(out_ref.at[:, tile], out_hbm.at[:, tile], sems.at[part])
        )
        copies[-1].start()
    for copy in copies:
        copy.wait()


def combine(pick, weights, rows):
    toks = weights.shape[0]
    slots, width = rows.shape
    held = pl.BlockSpec(memory_space=pltpu.VMEM)
    return pl.pallas_call(
        combine_kernel,
        in_specs=[held] * 3,
        out_specs=pl.BlockSpec(memory_space=pltpu.HBM),
        out_shape=pltpu.HBM((toks, width), BF16),
        scratch_shapes=[pltpu.VMEM((toks, width), BF16), pltpu.SemaphoreType.DMA((PARTS,))],
        compiler_params=pltpu.CompilerParams(vmem_limit_bytes=16 * 2**20),
        cost_estimate=pl.CostEstimate(
            flops=4 * toks * slots * width, bytes_accessed=2 * slots * width, transcendentals=0
        ),
        name="combine",
    )(pick, weights, rows)


def add_round(value, size, step, partner):
    stride = 2 * step
    pairs = [
        (i, partner[i // stride] * stride + i % stride) for i in range(size) if (i // step) % 2 == 1
    ]
    return value + lax.ppermute(value, AXES, pairs)


def on_device(tokens, expert_ids, gate_weights, w_gate, w_up, w_down):
    toks, width = tokens.shape
    picks = expert_ids.shape[1]
    group = lax.axis_size("expert")
    copies = lax.axis_size("dp")
    experts = w_gate.shape[0] * group
    cap = min(toks * picks // 4, 3 * toks * picks // experts)
    all_tokens = toks * group * copies

    size = copies * group
    ids, gates = expert_ids.T, gate_weights.T
    slots, stats, tokens, gates = count(ids, gates, tokens, experts, cap)
    swap = [(i, i + group if (i // group) % 2 == 0 else i - group) for i in range(size)]
    late = lax.axis_index("dp") % 2
    other = lax.ppermute(stats, AXES, swap)
    outgoing = pack(slots, tokens, experts * cap)

    def column_sum(value, other, rows):
        value = value + other
        for partner in ROUNDS:
            value = add_round(value, size, group, partner)
        return note(slots, value, rows, experts, cap)

    outgoing = lax.cond(late == 1, column_sum, lambda value, other, rows: rows, stats, other, outgoing)
    received = lax.all_to_all(outgoing, "expert", split_axis=0, concat_axis=0, tiled=True)
    slots, received = lax.optimization_barrier((slots, received))
    pick, weights = select(slots, gates, experts * cap)
    received, pick, weights = lax.optimization_barrier((received, pick, weights))
    hidden, loss = hidden_of(slots, received, w_gate, w_up, experts, cap, all_tokens)
    result = down_of(slots, loss, hidden, w_down, cap)
    returned = lax.all_to_all(result, "expert", split_axis=0, concat_axis=0, tiled=True)
    loss = read(slots, returned, cap)
    other = lax.ppermute(loss, AXES, swap)
    mixed = combine(pick, weights, returned)
    other, mixed = lax.optimization_barrier((other, mixed))
    return mixed, loss_of(loss, other).reshape(())


def solution(mesh):
    rows = P(("dp", "expert"), None)
    held = P("expert", None, None)
    return jax.shard_map(
        on_device,
        mesh=mesh,
        in_specs=(rows, rows, rows, held, held, held),
        out_specs=(rows, P()),
        check_vma=False,
    )
```
